32 devices in a mesh: dp: 8 (over z, y), tensor: 4 (over x, core).
Axes of the slice: x: 2, y: 2, z: 4, core: 2. Of those that a mesh axis runs over, the one named last changes fastest.
Arguments:
- hidden: bfloat16 [4096, 11008], P('dp', 'tensor'), may hold values from -6 to 6
- next_hidden: bfloat16 [4096, 11008], P('dp', 'tensor'), may hold values from -6 to 6
- out_grad: bfloat16 [4096, 4096], P('dp'), may hold values from -0.09375 to 0.09375
- sign_bits: int32 [16, 256], replicated, may hold values from 0 to 1
- scale_index: int32 [11008, 16], P('tensor'), may hold values from 0 to 3
- master: float32 [11008, 4096], P(('tensor', 'dp')), may hold values from -0.0546875 to 0.0546875
- moment_one: float32 [11008, 4096], P(('tensor', 'dp')), may hold values from -1.5 to 1.5
- moment_two: float32 [11008, 4096], P(('tensor', 'dp')), may hold values from 0.01 to 1
Outputs:
- gradient: float32 [11008, 4096], P(('tensor', 'dp'))
- new_master: float32 [11008, 4096], P(('tensor', 'dp'))
- new_moment_one: float32 [11008, 4096], P(('tensor', 'dp'))
- new_moment_two: float32 [11008, 4096], P(('tensor', 'dp'))
- next_out: bfloat16 [4096, 4096], P(('dp', 'tensor'))
The draws below stay inside these ranges and needn't reach their ends.
All inputs are finite; a program needn't handle non-finite values.
Results may differ from the reference program's by a relative error of at most 0.023.
Values may be sent and summed in bfloat16 or wider, within the bound.
No kernel may reach another device: no remote copies, remote signals or barrier semaphores. Data moves between devices by JAX's collectives and lax.ppermute only.
A program may use at most 192 MiB of HBM per device.

```python
import math
import jax
import jax.numpy as jnp
from jax import lax

D = 4096
FF = 11008
BLOCK = 256
TOK_DEV = 512
TOKENS = 4096
N_DP = 8
N_TENSOR = 4


def place_ends(entries, rng, least, top_value):
    spot = [jax.random.randint(jax.random.fold_in(rng, axis), (), 0, length) for axis, length in enumerate(entries.shape)]
    longest = entries.shape.index(max(entries.shape))
    beside = spot[:longest] + [(spot[longest] + 1) % entries.shape[longest]] + spot[longest + 1:]
    return entries.at[tuple(spot)].set(least).at[tuple(beside)].set(top_value)


def with_spikes(values, stream_key, source, target, shards_of, factor):
    owner, partner = [(jnp.arange(values.shape[dim]) // (values.shape[dim] // shards_of)).reshape([-1 if axis == dim else 1 for axis in range(values.ndim)]) for dim in (source, target)]
    chosen = jax.random.permutation(stream_key, shards_of)[partner]
    strong = (owner == chosen) | (owner == (partner + shards_of // 2) % shards_of)
    return jnp.where(strong, factor * values, values)


def steps_of(stream_key, dims, pieces, least, largest):
    level, own = 1.0, jax.random.fold_in(stream_key, 6)
    for position, shards_of in pieces:
        steps = jnp.exp(jax.random.uniform(jax.random.fold_in(own, position), (shards_of,), jnp.float32, least / len(pieces), largest / len(pieces)))
        level = level * jnp.repeat(steps, dims[position] // shards_of).reshape([-1 if axis == position else 1 for axis in range(len(dims))])
    return level


def centred(stream_key, extent, scale, reach, split=(), kind=jnp.bfloat16):
    gain = steps_of(stream_key, extent, split, -0.22, 0.18) if split else 1.0
    drawn = jax.random.normal(stream_key, extent, jnp.float32) * scale * gain
    return jnp.minimum(jnp.maximum(drawn, -reach), reach).astype(kind)


def noise_with(own_key, dims, width, bound, pieces, heavy, kind=jnp.bfloat16):
    entries = width * jax.random.normal(own_key, dims, jnp.float32)
    if pieces:
        entries = entries * steps_of(own_key, dims, pieces, -0.22, 0.18)
    return jnp.clip(with_spikes(entries, jax.random.fold_in(own_key, 3), *heavy), -bound, bound).astype(kind)


def setup_inputs(seed: int = 0) -> dict:
    arg_keys = jax.random.split(jax.random.key(seed), 9)
    return {
        "hidden": noise_with(arg_keys[0], (TOKENS, FF), 1.0, 6.0, ((0, 8), (1, 4)), (0, 1, 8, 2.0)),
        "next_hidden": centred(arg_keys[1], (TOKENS, FF), 1.0, 6.0, ((0, 8), (1, 4))),
        "out_grad": centred(arg_keys[2], (TOKENS, D), TOKENS ** -0.5, 0.09375, ((0, 8),)),
        "sign_bits": place_ends(jax.random.randint(arg_keys[3], (D // BLOCK, BLOCK), 0, 2), jax.random.fold_in(arg_keys[3], 1), 0, 1).astype(jnp.int32),
        "scale_index": place_ends(jax.random.randint(arg_keys[4], (FF, D // BLOCK), 0, 4), jax.random.fold_in(arg_keys[4], 1), 0, 3).astype(jnp.int32),
        "master": centred(arg_keys[5], (FF, D), FF ** -0.5, 0.0546875, ((0, 32),), jnp.float32),
        "moment_one": centred(arg_keys[6], (FF, D), 0.1, 1.5, ((0, 32),), jnp.float32),
        "moment_two": jnp.clip(jnp.exp(math.log(1.0) - 4.6051702 * jax.random.uniform(arg_keys[7], (FF, D), jnp.float32) ** steps_of(arg_keys[7], (FF, D), ((0, 32),), -0.2, 0.2)), 0.01, 1.0),
    }


CLIP_LEVEL = 127.0
LEARN_RATE = 0.005
BETA_ONE = 0.9
BETA_TWO = 0.95
WEIGHT_DECAY = 0.1
EPSILON = 1e-08
FIRST_BIAS = 1.0 - (0.9 ** 50) ** 2
SECOND_BIAS = 1.0 - (0.95 ** 50) ** 2
LEVELS = (16.0, 32.0, 64.0, 128.0)

def hadamard(block_size):
    positions = jnp.arange(block_size, dtype=jnp.int32)
    common_bits = jnp.bitwise_and(positions[:, None], positions[None, :])
    parity = jnp.zeros((block_size, block_size), jnp.int32)
    for bit_shift in range(block_size.bit_length() - 1):
        parity = parity + jnp.bitwise_and(jnp.right_shift(common_bits, bit_shift), 1)
    return (1 - 2 * jnp.bitwise_and(parity, 1)).astype(jnp.float32) / math.sqrt(block_size)

def reference(hidden, next_hidden, out_grad, sign_bits, scale_index, master, moment_one, moment_two):
    matrix = hadamard(BLOCK)
    block_count = D // BLOCK
    sign_flips = (1 - 2 * sign_bits).astype(jnp.float32)
    signed = out_grad.astype(jnp.float32).reshape(TOKENS, block_count, BLOCK) * sign_flips
    rotated = jnp.einsum('tbj,jk->tbk', signed, matrix, precision=lax.Precision.HIGHEST)
    rotated = rotated.astype(jnp.bfloat16).reshape(TOKENS, D)
    level_table = jnp.array(LEVELS, jnp.float32)
    matches = (scale_index[:, :, None] == jnp.arange(4, dtype=jnp.int32)).astype(jnp.float32)
    scales = lax.optimization_barrier(jnp.sum(matches * level_table, axis=-1)) * math.sqrt(N_DP)
    hidden_groups = hidden.reshape(N_DP, TOK_DEV, FF)
    grad_groups = rotated.reshape(N_DP, TOK_DEV, D)

    def add_device(running, device_pair):
        tokens_hidden, tokens_grad = device_pair
        product = jnp.dot(tokens_hidden.T, tokens_grad, preferred_element_type=jnp.float32)
        scaled = product.reshape(FF, block_count, BLOCK) * scales[:, :, None]
        coded_terms = lax.optimization_barrier(jnp.clip(scaled, -CLIP_LEVEL, CLIP_LEVEL).astype(jnp.bfloat16))
        return (running + coded_terms.astype(jnp.float32).reshape(FF, D), None)
    summed, unused = lax.scan(add_device, jnp.zeros((FF, D), jnp.float32), (hidden_groups, grad_groups))
    unscaled = summed.reshape(FF, block_count, BLOCK) / scales[:, :, None]
    decoded = jnp.einsum('rbj,jk->rbk', unscaled, matrix, precision=lax.Precision.HIGHEST)
    gradient = (decoded * sign_flips).reshape(FF, D)
    new_one = BETA_ONE * moment_one + (1.0 - BETA_ONE) * gradient
    new_two = BETA_TWO * moment_two + (1.0 - BETA_TWO) * gradient * gradient
    update = new_one / FIRST_BIAS / (jnp.sqrt(new_two / SECOND_BIAS) + EPSILON)
    new_master = master - LEARN_RATE * (update + WEIGHT_DECAY * master)
    new_weight = new_master.astype(jnp.bfloat16)
    group_units = FF // N_TENSOR
    input_groups = jnp.transpose(next_hidden.reshape(TOKENS, N_TENSOR, group_units), (1, 0, 2))
    weight_groups = new_weight.reshape(N_TENSOR, group_units, D)

    def add_group(running, group_pair):
        inputs, weights = group_pair
        partial_value = jnp.dot(inputs, weights, preferred_element_type=jnp.float32)
        rounded = lax.optimization_barrier(partial_value.astype(jnp.bfloat16))
        return (running + rounded.astype(jnp.float32), None)
    totals, unused_too = lax.scan(add_group, jnp.zeros((TOKENS, D), jnp.float32), (input_groups, weight_groups))
    next_out = totals.astype(jnp.bfloat16)
    return (gradient, new_master, new_one, new_two, next_out)
```

```python
import math

import jax
import jax.numpy as jnp
import numpy as np
from jax import lax
from jax.experimental import pallas as pl
from jax.experimental.pallas import tpu as pltpu
from jax.sharding import PartitionSpec as P

BLOCK = 256


CLIP_LEVEL = 127.0
LEARN_RATE = 0.005
BETA_ONE = 0.9
BETA_TWO = 0.95
WEIGHT_DECAY = 0.1
EPSILON = 1e-08
FIRST_BIAS = 1.0 - (0.9**50) ** 2
SECOND_BIAS = 1.0 - (0.95**50) ** 2
LEVELS = (16.0, 32.0, 64.0, 128.0)
CHUNKS = 4
VMEM_BYTES = 40 * 1024 * 1024


def hadamard(block_size):
    positions = np.arange(block_size)
    common_bits = positions[:, None] & positions[None, :]
    parity = np.zeros((block_size, block_size), np.int32)
    for bit_shift in range(block_size.bit_length() - 1):
        parity += (common_bits >> bit_shift) & 1
    return ((1 - 2 * (parity & 1)) / math.sqrt(block_size)).astype(np.float32)


def dot(a, b):
    return lax.dot_general(a, b, (((1,), (0,)), ((), ())), preferred_element_type=jnp.float32)


def block_spec(shape, index_map):
    return pl.BlockSpec(shape, index_map)


def kernel_call(body, grid, in_specs, out_specs, out_shape, scratch, flops, aliases=None):
    total = sum(math.prod(s.shape) * s.dtype.itemsize for s in out_shape)
    return pl.pallas_call(
        body,
        grid_spec=pltpu.PrefetchScalarGridSpec(
            num_scalar_prefetch=1,
            grid=grid,
            in_specs=in_specs,
            out_specs=out_specs,
            scratch_shapes=scratch,
        ),
        out_shape=out_shape,
        input_output_aliases=aliases or {},
        compiler_params=pltpu.CompilerParams(vmem_limit_bytes=VMEM_BYTES),
        cost_estimate=pl.CostEstimate(flops=flops, bytes_accessed=2 * total, transcendentals=0),
    )


def rotate(place, out_grad, flips, matrix):
    rows, width = out_grad.shape

    def body(place_ref, grad_ref, flips_ref, matrix_ref, out_ref):
        signed = grad_ref[...] * flips_ref[0]
        out_ref[...] = dot(signed, matrix_ref[...]).astype(jnp.bfloat16)

    return kernel_call(
        body,
        (width // BLOCK,),
        [
            block_spec((rows, BLOCK), lambda b, p: (0, b)),
            block_spec((1, 1, BLOCK), lambda b, p: (b, 0, 0)),
            block_spec((BLOCK, BLOCK), lambda b, p: (0, 0)),
        ],
        [block_spec((rows, BLOCK), lambda b, p: (0, b))],
        [jax.ShapeDtypeStruct((rows, width), jnp.bfloat16)],
        [],
        2 * rows * width * BLOCK,
    )(place, out_grad, flips.reshape(width // BLOCK, 1, BLOCK), matrix)[0]


def coded_sum(place, chunk, hidden_parts, rotated, pieces, scales):
    units, tokens = hidden_parts[0].shape
    rows = units // 2
    width = rotated.shape[1] // CHUNKS
    piece = width // 4
    block_count = scales.shape[1]

    def body(place_ref, h0, h1, h2, h3, own_ref, u_ref, cu_ref, v_ref, cv_ref, scales_ref, keep_ref, send_ref, acc_ref):
        position = place_ref[0]
        start = pl.multiple_of(place_ref[1] * rows, 8)
        other = pl.multiple_of((1 - place_ref[1]) * rows, 8)
        lane = lax.broadcasted_iota(jnp.int32, (units, block_count), 1)
        all_scales = scales_ref[...]
        for j, ref in enumerate((u_ref, cu_ref, v_ref, cv_ref)):
            quarter = jnp.bitwise_xor(position, j)
            for part in range(piece // BLOCK):
                column = pl.multiple_of(quarter * piece + part * BLOCK, BLOCK)
                columns = pl.ds(column, BLOCK)
                block = chunk * (width // BLOCK) + quarter * (piece // BLOCK) + part
                scale = jnp.sum(jnp.where(lane == block, all_scales, 0.0), axis=1, keepdims=True)

                def coded(hidden, values):
                    product = dot(hidden, values) * scale
                    return jnp.clip(product, -CLIP_LEVEL, CLIP_LEVEL).astype(jnp.bfloat16).astype(jnp.float32)

                total = coded(h0[...], own_ref[:, columns])
                for k, hidden_ref in enumerate((h1, h2, h3)):
                    total = total + coded(hidden_ref[...], ref[k, :, part * BLOCK : (part + 1) * BLOCK])
                acc_ref[...] = total
                keep_ref[:, columns] = acc_ref[pl.ds(start, rows), :].astype(jnp.bfloat16)
                send_ref[:, columns] = acc_ref[pl.ds(other, rows), :].astype(jnp.bfloat16)

    whole = lambda shape: block_spec(shape, lambda i, p: (0,) * len(shape))
    out = jax.ShapeDtypeStruct((rows, width), jnp.bfloat16)
    return kernel_call(
        body,
        (1,),
        [whole((units, tokens))] * 4
        + [block_spec((tokens, width), lambda i, p: (0, chunk))]
        + [whole((3, tokens, piece))] * 4
        + [whole((units, block_count))],
        [whole((rows, width))] * 2,
        [out, out],
        [pltpu.VMEM((units, BLOCK), jnp.float32)],
        8 * units * tokens * width,
    )(place, *hidden_parts, rotated, *pieces, scales)


def adam(place, chunk, kept, received, shard_scales, flips, matrix, master, one, two, previous):
    rows, width = kept.shape
    model_width = master.shape[1]
    block_count = shard_scales.shape[1]
    per_chunk = width // BLOCK
    chained = previous is not None

    def body(place_ref, kept_ref, received_ref, scales_ref, flips_ref, matrix_ref, master_ref, one_ref, two_ref, *rest):
        grad_out, master_out, one_out, two_out, weight_out = rest[-5:]
        block = chunk * per_chunk + pl.program_id(0)
        lane = lax.broadcasted_iota(jnp.int32, (rows, block_count), 1)
        scale = jnp.sum(jnp.where(lane == block, scales_ref[...], 0.0), axis=1, keepdims=True)
        decoded = dot(kept_ref[...], matrix_ref[...]) + dot(received_ref[...], matrix_ref[...])
        gradient = decoded / scale * flips_ref[0]
        new_one = BETA_ONE * one_ref[...] + (1.0 - BETA_ONE) * gradient
        new_two = BETA_TWO * two_ref[...] + (1.0 - BETA_TWO) * gradient * gradient
        update = new_one / FIRST_BIAS / (jnp.sqrt(new_two / SECOND_BIAS) + EPSILON)
        old = master_ref[...]
        new_master = old - LEARN_RATE * (update + WEIGHT_DECAY * old)
        grad_out[...] = gradient
        master_out[...] = new_master
        one_out[...] = new_one
        two_out[...] = new_two
        weight_out[...] = new_master.astype(jnp.bfloat16)

    local = block_spec((rows, BLOCK), lambda j, p: (0, j))
    placed = block_spec((rows, BLOCK), lambda j, p: (0, chunk * per_chunk + j))
    state = jax.ShapeDtypeStruct((rows, model_width), jnp.float32)
    return kernel_call(
        body,
        (per_chunk,),
        [
            local,
            local,
            block_spec((rows, block_count), lambda j, p: (0, 0)),
            block_spec((1, 1, BLOCK), lambda j, p: (chunk * per_chunk + j, 0, 0)),
            block_spec((BLOCK, BLOCK), lambda j, p: (0, 0)),
            placed,
            placed,
            placed,
        ]
        + ([pl.BlockSpec(memory_space=pl.ANY)] * 4 if chained else []),
        [placed] * 4 + [local],
        [state] * 4 + [jax.ShapeDtypeStruct((rows, width), jnp.bfloat16)],
        [],
        4 * rows * width * BLOCK,
        {9 + i: i for i in range(4)} if chained else None,
    )(
        place,
        kept,
        received,
        shard_scales,
        flips.astype(jnp.float32).reshape(block_count, 1, BLOCK),
        matrix,
        master,
        one,
        two,
        *(previous if chained else ()),
    )


def forward(place, inputs, weights):
    tokens, units = inputs[0].shape
    width = weights.shape[1]
    quarter = tokens // 4

    def body(place_ref, n0, n1, n2, n3, weight_ref, keep_ref, send_ref, acc_ref):
        position = place_ref[0]
        weight = weight_ref[...]
        for k, ref in enumerate((n0, n1, n2, n3)):
            acc_ref[...] = dot(ref[...], weight).astype(jnp.bfloat16)
            for i in range(2):
                mine = jnp.bitwise_xor(position, 2 * i)
                theirs = jnp.bitwise_xor(position, 2 * i + 1)
                keep_ref[k, i] = acc_ref[pl.ds(pl.multiple_of(mine * quarter, quarter), quarter), :]
                send_ref[k, i] = acc_ref[pl.ds(pl.multiple_of(theirs * quarter, quarter), quarter), :]

    out = jax.ShapeDtypeStruct((4, 2, quarter, width), jnp.bfloat16)
    placed = block_spec((4, 2, quarter, BLOCK), lambda j, p: (0, 0, 0, j))
    return kernel_call(
        body,
        (width // BLOCK,),
        [block_spec((tokens, units), lambda j, p: (0, 0))] * 4 + [block_spec((units, BLOCK), lambda j, p: (0, j))],
        [placed, placed],
        [out, out],
        [pltpu.VMEM((tokens, BLOCK), jnp.bfloat16)],
        8 * tokens * units * width,
    )(place, *inputs, weights)


def add(a, b):
    return (a.astype(jnp.float32) + b.astype(jnp.float32)).astype(jnp.bfloat16)


def on_device(
    hidden, next_hidden, out_grad, sign_bits, scale_index, master, moment_one, moment_two
):
    dp_size = lax.axis_size("dp")
    tensor_size = lax.axis_size("tensor")
    model_width = out_grad.shape[1]
    shard_rows = master.shape[0]
    block_count = sign_bits.shape[0]
    replica = lax.axis_index("dp")
    group = lax.axis_index("tensor")
    z, y = replica // 2, replica % 2
    place = jnp.stack([group, y]).astype(jnp.int32)
    matrix = jnp.asarray(hadamard(BLOCK)).astype(jnp.bfloat16)
    flips = (1 - 2 * sign_bits).astype(jnp.bfloat16)

    def over_dp(value, bits):
        return lax.ppermute(value, "dp", [(i, i ^ bits) for i in range(dp_size)])

    def over_tensor(value, bits):
        return lax.ppermute(value, "tensor", [(i, i ^ bits) for i in range(tensor_size)])

    units = 2 * shard_rows
    hidden_t = hidden.T
    hidden_parts = [lax.dynamic_slice_in_dim(hidden_t, (z ^ k) * units, units, 0) for k in range(4)]
    hidden_parts = [hidden_parts[0]] + [over_dp(hidden_parts[k], 2 * k) for k in range(1, 4)]
    level_table = jnp.array(LEVELS, jnp.float32)
    own_index = lax.dynamic_slice_in_dim(scale_index, z * units, units, 0)
    matches = (own_index[:, :, None] == jnp.arange(4, dtype=jnp.int32)).astype(jnp.float32)
    scales = jnp.sum(matches * level_table, axis=-1) * math.sqrt(dp_size)
    shard_scales = lax.dynamic_slice_in_dim(scales, y * shard_rows, shard_rows, 0)

    rotated = rotate(place, out_grad, flips, matrix)
    width = model_width // CHUNKS
    piece = width // 4

    gathered = []
    for chunk in range(CHUNKS):
        u0 = lax.dynamic_slice_in_dim(rotated, chunk * width + group * piece, piece, 1)
        u2 = over_dp(u0, 4)
        u1 = over_dp(u0, 2)
        u3 = over_dp(u2, 2)
        u = jnp.stack([u1, u2, u3])
        v = over_tensor(u, 2)
        gathered.append((u, over_tensor(u, 1), v, over_tensor(v, 1)))

    inputs = [lax.dynamic_slice_in_dim(next_hidden, (z ^ k) * units, units, 1) for k in range(4)]
    inputs = [inputs[0]] + [over_dp(inputs[k], 2 * k) for k in range(1, 4)]

    state = None
    outs = []
    for chunk in range(CHUNKS):
        kept, sent = coded_sum(place, chunk, hidden_parts, rotated, gathered[chunk], scales)
        *state, weight = adam(
            place, chunk, kept, over_dp(sent, 1), shard_scales, flips, matrix, master, moment_one, moment_two, state
        )
        other = over_dp(weight, 1)
        weights = jnp.where(y == 0, jnp.concatenate([weight, other]), jnp.concatenate([other, weight]))
        keep, send = forward(place, inputs, weights)
        by_core = add(keep, over_tensor(send, 1))
        by_chip = add(by_core[:, 0], over_tensor(by_core[:, 1], 2))
        near = over_dp(jnp.stack([by_chip[1], by_chip[3]]), 2)
        own = add(by_chip[0], near[0])
        far = add(by_chip[2], near[1])
        outs.append(add(own, over_dp(far, 4)))
    gradient, new_master, new_one, new_two = state
    return (gradient, new_master, new_one, new_two, jnp.concatenate(outs, axis=1))


def general(
    hidden, next_hidden, out_grad, sign_bits, scale_index, master, moment_one, moment_two
):
    dp_size = lax.axis_size("dp")
    tok_rows = hidden.shape[0]
    model_width = out_grad.shape[1]
    block_count = sign_bits.shape[0]
    shard_rows = master.shape[0]
    matrix = jnp.asarray(hadamard(BLOCK))
    sign_flips = (1 - 2 * sign_bits).astype(jnp.float32)
    signed = out_grad.reshape(tok_rows, block_count, BLOCK) * sign_flips.astype(jnp.bfloat16)
    rotated = jnp.einsum(
        "tbj,jk->tbk", signed, matrix.astype(jnp.bfloat16), preferred_element_type=jnp.float32
    )
    rotated = rotated.astype(jnp.bfloat16).reshape(tok_rows, model_width)
    level_table = jnp.array(LEVELS, jnp.float32)
    matches = (scale_index[:, :, None] == jnp.arange(4, dtype=jnp.int32)).astype(jnp.float32)
    scales = jnp.sum(matches * level_table, axis=-1) * math.sqrt(dp_size)
    product = lax.dot_general(
        hidden, rotated, (((0,), (0,)), ((), ())), preferred_element_type=jnp.float32
    )
    scaled = product.reshape(dp_size * shard_rows, block_count, BLOCK) * scales[:, :, None]
    summed = lax.psum_scatter(
        jnp.clip(scaled, -CLIP_LEVEL, CLIP_LEVEL)
        .reshape(dp_size * shard_rows, model_width)
        .astype(jnp.bfloat16),
        "dp",
        scatter_dimension=0,
        tiled=True,
    ).astype(jnp.float32)
    shard_scales = lax.dynamic_slice_in_dim(
        scales, lax.axis_index("dp") * shard_rows, shard_rows, 0
    )
    unscaled = summed.reshape(shard_rows, block_count, BLOCK) / shard_scales[:, :, None]
    decoded = jnp.einsum("rbj,jk->rbk", unscaled, matrix, precision=lax.Precision.HIGHEST)
    gradient = (decoded * sign_flips).reshape(shard_rows, model_width)
    new_one = BETA_ONE * moment_one + (1.0 - BETA_ONE) * gradient
    new_two = BETA_TWO * moment_two + (1.0 - BETA_TWO) * gradient * gradient
    update = new_one / FIRST_BIAS / (jnp.sqrt(new_two / SECOND_BIAS) + EPSILON)
    new_master = master - LEARN_RATE * (update + WEIGHT_DECAY * master)
    partial_value = jnp.dot(
        next_hidden,
        lax.all_gather(new_master.astype(jnp.bfloat16), "dp", axis=0, tiled=True),
        preferred_element_type=jnp.float32,
    )
    next_out = lax.psum_scatter(
        partial_value.astype(jnp.bfloat16), "tensor", scatter_dimension=0, tiled=True
    )
    return (gradient, new_master, new_one, new_two, next_out)


def solution(mesh):
    grouped = mesh.shape["dp"] == 8 and mesh.shape["tensor"] == 4
    return jax.shard_map(
        on_device if grouped else general,
        mesh=mesh,
        in_specs=(
            P("dp", "tensor"),
            P("dp", "tensor"),
            P("dp", None),
            P(),
            P("tensor", None),
            P(("tensor", "dp"), None),
            P(("tensor", "dp"), None),
            P(("tensor", "dp"), None),
        ),
        out_specs=(
            P(("tensor", "dp"), None),
            P(("tensor", "dp"), None),
            P(("tensor", "dp"), None),
            P(("tensor", "dp"), None),
            P(("dp", "tensor"), None),
        ),
        check_vma=False,
    )
```

```python
import math

import jax
import jax.numpy as jnp
import numpy as np
from jax import lax
from jax.experimental import pallas as pl
from jax.experimental.pallas import tpu as pltpu
from jax.sharding import PartitionSpec as P

BLOCK = 256


CLIP_LEVEL = 127.0
LEARN_RATE = 0.005
BETA_ONE = 0.9
BETA_TWO = 0.95
WEIGHT_DECAY = 0.1
EPSILON = 1e-08
FIRST_BIAS = 1.0 - (0.9**50) ** 2
SECOND_BIAS = 1.0 - (0.95**50) ** 2
LEVELS = (16.0, 32.0, 64.0, 128.0)
CHUNKS = 4
GROUPS = 2
ADAM_STEPS = 2
FORWARD_STEPS = 2
ORDER = (
    "rot",
    "tu0",
    "g10",
    "tu3",
    "g11",
    "tu2",
    "g12",
    "ay0",
    "g13",
    "ay1",
    "ad0",
    "tu1",
    "ay2",
    "ad1",
    "g20",
    "ay3",
    "ad2",
    "g21",
    "sc0",
    "ad3",
    "g22",
    "sc1",
    "sx0",
    "g23",
    "sc2",
    "sx1",
    "sn0",
    "sc3",
    "sx2",
    "sn1",
    "sx3",
    "sn2",
    "sn3",
)
COST = {"ro": 1000000000, "st": 25000000000, "ay": 1000000000, "g1": 1000000000, "ad": 1000000000, "tu": 1000000000, "g2": 1000000000, "sc": 1000000000, "sx": 1000000000, "sn": 1000000000}
VMEM_BYTES = 28 * 1024 * 1024


def hadamard(block_size):
    positions = np.arange(block_size)
    common_bits = positions[:, None] & positions[None, :]
    parity = np.zeros((block_size, block_size), np.int32)
    for bit_shift in range(block_size.bit_length() - 1):
        parity += (common_bits >> bit_shift) & 1
    return ((1 - 2 * (parity & 1)) / math.sqrt(block_size)).astype(np.float32)


def dot(a, b):
    return lax.dot_general(a, b, (((1,), (0,)), ((), ())), preferred_element_type=jnp.float32)


def block_spec(shape, index_map):
    return pl.BlockSpec(shape, index_map)


def whole(shape):
    return pl.BlockSpec(shape, lambda i, p: (0,) * len(shape))


class Chain:
    def __init__(self, place):
        self.place = place
        self.held = []

    def note(self, value):
        self.held.append(value)

    def __call__(self, name, body, grid, in_specs, out_specs, out_shape, scratch, args, aliases=None, token=0):
        held = self.held
        count, extra = len(args), len(held)

        def wrapped(place_ref, *refs):
            body(place_ref, *refs[:count], *refs[count + extra :])

        outs = pl.pallas_call(
            wrapped,
            grid_spec=pltpu.PrefetchScalarGridSpec(
                num_scalar_prefetch=1,
                grid=grid,
                in_specs=list(in_specs) + [pl.BlockSpec(memory_space=pl.ANY)] * extra,
                out_specs=out_specs,
                scratch_shapes=scratch,
            ),
            out_shape=out_shape,
            input_output_aliases=aliases or {},
            compiler_params=pltpu.CompilerParams(vmem_limit_bytes=VMEM_BYTES),
            cost_estimate=pl.CostEstimate(flops=COST[name[:2]], bytes_accessed=1000, transcendentals=0),
        )(self.place, *args, *held)
        self.held = [outs[token]]
        return outs


def rotate(chain, out_grad, flips, matrix):
    rows, width = out_grad.shape
    step = width // CHUNKS
    piece = step // 4
    per_group = CHUNKS // GROUPS

    def body(place_ref, grad_ref, flips_ref, matrix_ref, out_ref, *own_refs):
        position = place_ref[0]
        for block in range(step // BLOCK):
            columns = slice(block * BLOCK, (block + 1) * BLOCK)
            signed = grad_ref[:, columns] * flips_ref[block]
            out_ref[:, columns] = dot(signed, matrix_ref[...]).astype(jnp.bfloat16)
        for chunk in range(CHUNKS):

            @pl.when(pl.program_id(0) == chunk)
            def _():
                start = (chunk % per_group) * piece
                own = out_ref[:, pl.ds(pl.multiple_of(position * piece, BLOCK), piece)]
                own_refs[chunk // per_group][:, start : start + piece] = own

    return chain(
        "rot",
        body,
        (CHUNKS,),
        [
            block_spec((rows, step), lambda b, p: (0, b)),
            block_spec((step // BLOCK, 1, BLOCK), lambda b, p: (b, 0, 0)),
            whole((BLOCK, BLOCK)),
        ],
        [block_spec((rows, step), lambda b, p: (0, b))] + [whole((rows, per_group * piece))] * GROUPS,
        [jax.ShapeDtypeStruct((rows, width), jnp.bfloat16)]
        + [jax.ShapeDtypeStruct((rows, per_group * piece), jnp.bfloat16)] * GROUPS,
        [],
        (out_grad, flips.reshape(width // BLOCK, 1, BLOCK), matrix),
    )


def coded_sum(chain, chunk, hidden_parts, rotated, pieces, scales):
    units, tokens = hidden_parts[0].shape
    rows = units // 4
    width = rotated.shape[1] // CHUNKS
    piece = width // 4
    block_count = scales.shape[1]

    def body(place_ref, h0, h1, own_ref, u_ref, cu_ref, v_ref, cv_ref, scales_ref, keep_ref, send_ref, acc_ref):
        position, y = place_ref[0], place_ref[1]
        mine = pl.ds(pl.multiple_of(y * rows, 8), rows)
        theirs = pl.ds(pl.multiple_of((1 - y) * rows, 8), rows)
        lane = lax.broadcasted_iota(jnp.int32, (2 * rows, block_count), 1)
        all_scales = scales_ref[...]
        for j, ref in enumerate((u_ref, cu_ref, v_ref, cv_ref)):
            quarter = jnp.bitwise_xor(position, j)
            for part in range(piece // BLOCK):
                column = pl.multiple_of(quarter * piece + part * BLOCK, BLOCK)
                columns = pl.ds(column, BLOCK)
                block = chunk * (width // BLOCK) + quarter * (piece // BLOCK) + part
                scale = jnp.sum(jnp.where(lane == block, all_scales, 0.0), axis=1, keepdims=True)

                def coded(hidden, values):
                    product = dot(hidden, values) * scale
                    return jnp.clip(product, -CLIP_LEVEL, CLIP_LEVEL).astype(jnp.bfloat16).astype(jnp.float32)

                acc_ref[...] = coded(h0[...], own_ref[:, columns]) + coded(
                    h1[...], ref[:, part * BLOCK : (part + 1) * BLOCK]
                )
                keep_ref[0, :, columns] = acc_ref[mine, :].astype(jnp.bfloat16)
                send_ref[0, :, columns] = acc_ref[theirs, :].astype(jnp.bfloat16)

    out = jax.ShapeDtypeStruct((2, rows, width), jnp.bfloat16)
    part_spec = block_spec((tokens, piece), lambda i, p: (0, chunk % (CHUNKS // GROUPS)))
    return chain(
        f"g1{chunk}",
        body,
        (2,),
        [block_spec((2 * rows, tokens), lambda i, p: (i, 0))] * 2
        + [block_spec((tokens, width), lambda i, p: (0, chunk))]
        + [part_spec] * 4
        + [block_spec((2 * rows, block_count), lambda i, p: (i, 0))],
        [block_spec((1, rows, width), lambda i, p: (i, 0, 0))] * 2,
        [out, out],
        [pltpu.VMEM((2 * rows, BLOCK), jnp.float32)],
        (*hidden_parts, rotated, *pieces, scales),
    )


def adam(chain, chunk, kept, received, shard_scales, flips, matrix, master, one, two, previous):
    rows, width = kept.shape
    model_width = master.shape[1]
    block_count = shard_scales.shape[1]
    step = width // ADAM_STEPS
    parts = step // BLOCK
    chained = previous is not None

    def body(place_ref, kept_ref, received_ref, scales_ref, flips_ref, matrix_ref, master_ref, one_ref, two_ref, *rest):
        grad_out, master_out, one_out, two_out, weight_out = rest[-5:]
        lane = lax.broadcasted_iota(jnp.int32, (rows, block_count), 1)
        all_scales = scales_ref[...]
        for part in range(parts):
            block = (chunk * ADAM_STEPS + pl.program_id(0)) * parts + part
            columns = slice(part * BLOCK, (part + 1) * BLOCK)
            scale = jnp.sum(jnp.where(lane == block, all_scales, 0.0), axis=1, keepdims=True)
            decoded = dot(kept_ref[:, columns], matrix_ref[...]) + dot(received_ref[:, columns], matrix_ref[...])
            gradient = decoded / scale * flips_ref[part]
            new_one = BETA_ONE * one_ref[:, columns] + (1.0 - BETA_ONE) * gradient
            new_two = BETA_TWO * two_ref[:, columns] + (1.0 - BETA_TWO) * gradient * gradient
            update = new_one / FIRST_BIAS / (jnp.sqrt(new_two / SECOND_BIAS) + EPSILON)
            old = master_ref[:, columns]
            new_master = old - LEARN_RATE * (update + WEIGHT_DECAY * old)
            grad_out[:, columns] = gradient
            master_out[:, columns] = new_master
            one_out[:, columns] = new_one
            two_out[:, columns] = new_two
            weight_out[:, columns] = new_master.astype(jnp.bfloat16)

    local = block_spec((rows, step), lambda j, p: (0, j))
    placed = block_spec((rows, step), lambda j, p: (0, chunk * ADAM_STEPS + j))
    state = jax.ShapeDtypeStruct((rows, model_width), jnp.float32)
    return chain(
        f"ad{chunk}",
        body,
        (ADAM_STEPS,),
        [
            local,
            local,
            whole((rows, block_count)),
            block_spec((parts, 1, BLOCK), lambda j, p: (chunk * ADAM_STEPS + j, 0, 0)),
            whole((BLOCK, BLOCK)),
            placed,
            placed,
            placed,
        ]
        + ([pl.BlockSpec(memory_space=pl.ANY)] * 4 if chained else []),
        [placed] * 4 + [local],
        [state] * 4 + [jax.ShapeDtypeStruct((rows, width), jnp.bfloat16)],
        [],
        (
            kept,
            received,
            shard_scales,
            flips.astype(jnp.float32).reshape(block_count, 1, BLOCK),
            matrix,
            master,
            one,
            two,
            *(previous if chained else ()),
        ),
        {9 + i: i for i in range(4)} if chained else None,
        token=4,
    )


def forward(chain, name, inputs, weight, other):
    tokens, units = inputs[0].shape
    rows, width = weight.shape
    quarter = tokens // 4
    step = width // FORWARD_STEPS

    def body(place_ref, n0, n1, n2, n3, weight_ref, other_ref, o0, o1, o2, o3, acc_ref, joined_ref):
        position, y = place_ref[0], place_ref[1]
        joined_ref[pl.ds(pl.multiple_of(y * rows, 8), rows), :] = weight_ref[...].astype(jnp.float32)
        joined_ref[pl.ds(pl.multiple_of((1 - y) * rows, 8), rows), :] = other_ref[...].astype(jnp.float32)
        joined = joined_ref[...].astype(jnp.bfloat16)
        for k, ref in enumerate((n0, n2, n1, n3)):
            acc_ref[...] = dot(ref[...], joined).astype(jnp.bfloat16)
            for i, out_ref in enumerate((o0, o1, o2, o3)):
                start = jnp.bitwise_xor(position, i) * quarter
                out_ref[k] = acc_ref[pl.ds(pl.multiple_of(start, quarter), quarter), :]

    return chain(
        name,
        body,
        (FORWARD_STEPS,),
        [whole((tokens, units))] * 4 + [block_spec((rows, step), lambda j, p: (0, j))] * 2,
        [block_spec((4, quarter, step), lambda j, p: (0, 0, j))] * 4,
        [jax.ShapeDtypeStruct((4, quarter, width), jnp.bfloat16)] * 4,
        [pltpu.VMEM((tokens, step), jnp.bfloat16), pltpu.VMEM((units, step), jnp.float32)],
        (*inputs, weight, other),
    )


def add(a, b):
    return (a.astype(jnp.float32) + b.astype(jnp.float32)).astype(jnp.bfloat16)


def on_device(
    hidden, next_hidden, out_grad, sign_bits, scale_index, master, moment_one, moment_two
):
    dp_size = lax.axis_size("dp")
    tensor_size = lax.axis_size("tensor")
    tokens = hidden.shape[0]
    shard_rows = master.shape[0]
    block_count = sign_bits.shape[0]
    replica = lax.axis_index("dp")
    group = lax.axis_index("tensor")
    z, y = replica // 2, replica % 2
    far_side = replica // 4
    place = jnp.stack([group, y, far_side]).astype(jnp.int32)
    matrix = jnp.asarray(hadamard(BLOCK)).astype(jnp.bfloat16)
    flips = (1 - 2 * sign_bits).astype(jnp.bfloat16)

    def over_dp(value, bits):
        return lax.ppermute(value, "dp", [(i, i ^ bits) for i in range(dp_size)])

    def over_tensor(value, bits):
        return lax.ppermute(value, "tensor", [(i, i ^ bits) for i in range(tensor_size)])

    units = 2 * shard_rows
    near_z = z % 2
    by_pair = hidden.T.reshape(2, 2, units, tokens)

    def pair_rows(values, k):
        picked = lax.dynamic_index_in_dim(values, near_z ^ k, 1, keepdims=False)
        return picked.reshape(2 * units, picked.shape[-1])

    hidden_parts = [pair_rows(by_pair, 0), over_dp(pair_rows(by_pair, 1), 2)]
    chain = Chain(place)
    rotated, *own_pieces = rotate(chain, out_grad, flips, matrix)

    level_table = jnp.array(LEVELS, jnp.float32)
    matches = (scale_index[:, :, None] == jnp.arange(4, dtype=jnp.int32)).astype(jnp.float32)
    all_scales = jnp.sum(matches * level_table, axis=-1) * math.sqrt(dp_size)
    scales = pair_rows(all_scales.reshape(2, 2, units, block_count), 0)
    shard_scales = lax.dynamic_slice_in_dim(scales, (2 * far_side + y) * shard_rows, shard_rows, 0)

    next_t = next_hidden.T
    inputs = [lax.dynamic_slice_in_dim(next_t, (z ^ k) * units, units, 0) for k in range(4)]
    inputs = [inputs[0]] + [over_dp(inputs[k], 2 * k) for k in range(1, 4)]

    state = None
    pieces, kept, halves, arriving, weights, partials, sums, nears, outs = ({} for _ in range(9))
    turned_inputs = {}

    def gather(k):
        u = over_dp(own_pieces[k], 2)
        v = over_tensor(u, 2)
        pieces[k] = (u, over_tensor(u, 1), v, over_tensor(v, 1))

    def first(k):
        kept[k], sent = coded_sum(chain, k, hidden_parts, rotated, pieces[k // (CHUNKS // GROUPS)], scales)
        halves[k] = over_dp(sent, 1)

    def join_rows(k):
        def side(value, index):
            return lax.dynamic_index_in_dim(value, index, 0, keepdims=False)

        go = add(side(kept[k], 1 - far_side), side(halves[k], 1 - far_side))
        kept[k] = add(side(kept[k], far_side), side(halves[k], far_side))
        arriving[k] = over_dp(go, 4)
        chain.note(go)

    def update(k):
        nonlocal state
        *state, weight = adam(
            chain, k, kept[k], arriving[k], shard_scales, flips, matrix, master, moment_one, moment_two, state
        )
        weights[k] = (weight, over_dp(weight, 1))

    def turn(k):
        turned_inputs[k] = inputs[k].T
        chain.note(inputs[k])

    def second(k):
        stay, near, go, far = forward(chain, f"g2{k}", [turned_inputs[i] for i in range(4)], *weights[k])
        partials[k] = (stay, go, over_tensor(near, 1), over_tensor(far, 1))

    def sum_cores(k):
        stay, go, near, far = partials[k]
        go = add(go, far)
        sums[k] = (add(stay, near), over_tensor(go, 2))
        chain.note(go)

    def sum_chips(k):
        stay, more = sums[k]
        go = add(stay[2:], more[2:])
        nears[k] = (add(stay[:2], more[:2]), over_dp(go, 2))
        chain.note(go)

    def sum_near(k):
        stay, more = nears[k]
        go = add(stay[1], more[1])
        outs[k] = (add(stay[0], more[0]), over_dp(go, 4))
        chain.note(go)

    steps = {"tu": turn, "ay": join_rows, "g1": first, "ad": update, "g2": second, "sc": sum_cores, "sx": sum_chips, "sn": sum_near}
    for group_index in range(GROUPS):
        gather(group_index)
    for name in ORDER[1:]:
        steps[name[:2]](int(name[2:]))
    next_out = jnp.concatenate([add(*outs[k]) for k in range(CHUNKS)], axis=1)
    gradient, new_master, new_one, new_two = state
    return (gradient, new_master, new_one, new_two, next_out)


def general(
    hidden, next_hidden, out_grad, sign_bits, scale_index, master, moment_one, moment_two
):
    dp_size = lax.axis_size("dp")
    tok_rows = hidden.shape[0]
    model_width = out_grad.shape[1]
    block_count = sign_bits.shape[0]
    shard_rows = master.shape[0]
    matrix = jnp.asarray(hadamard(BLOCK))
    sign_flips = (1 - 2 * sign_bits).astype(jnp.float32)
    signed = out_grad.reshape(tok_rows, block_count, BLOCK) * sign_flips.astype(jnp.bfloat16)
    rotated = jnp.einsum(
        "tbj,jk->tbk", signed, matrix.astype(jnp.bfloat16), preferred_element_type=jnp.float32
    )
    rotated = rotated.astype(jnp.bfloat16).reshape(tok_rows, model_width)
    level_table = jnp.array(LEVELS, jnp.float32)
    matches = (scale_index[:, :, None] == jnp.arange(4, dtype=jnp.int32)).astype(jnp.float32)
    scales = jnp.sum(matches * level_table, axis=-1) * math.sqrt(dp_size)
    product = lax.dot_general(
        hidden, rotated, (((0,), (0,)), ((), ())), preferred_element_type=jnp.float32
    )
    scaled = product.reshape(dp_size * shard_rows, block_count, BLOCK) * scales[:, :, None]
    summed = lax.psum_scatter(
        jnp.clip(scaled, -CLIP_LEVEL, CLIP_LEVEL)
        .reshape(dp_size * shard_rows, model_width)
        .astype(jnp.bfloat16),
        "dp",
        scatter_dimension=0,
        tiled=True,
    ).astype(jnp.float32)
    shard_scales = lax.dynamic_slice_in_dim(
        scales, lax.axis_index("dp") * shard_rows, shard_rows, 0
    )
    unscaled = summed.reshape(shard_rows, block_count, BLOCK) / shard_scales[:, :, None]
    decoded = jnp.einsum("rbj,jk->rbk", unscaled, matrix, precision=lax.Precision.HIGHEST)
    gradient = (decoded * sign_flips).reshape(shard_rows, model_width)
    new_one = BETA_ONE * moment_one + (1.0 - BETA_ONE) * gradient
    new_two = BETA_TWO * moment_two + (1.0 - BETA_TWO) * gradient * gradient
    update = new_one / FIRST_BIAS / (jnp.sqrt(new_two / SECOND_BIAS) + EPSILON)
    new_master = master - LEARN_RATE * (update + WEIGHT_DECAY * master)
    partial_value = jnp.dot(
        next_hidden,
        lax.all_gather(new_master.astype(jnp.bfloat16), "dp", axis=0, tiled=True),
        preferred_element_type=jnp.float32,
    )
    next_out = lax.psum_scatter(
        partial_value.astype(jnp.bfloat16), "tensor", scatter_dimension=0, tiled=True
    )
    return (gradient, new_master, new_one, new_two, next_out)


def solution(mesh):
    grouped = mesh.shape["dp"] == 8 and mesh.shape["tensor"] == 4
    return jax.shard_map(
        on_device if grouped else general,
        mesh=mesh,
        in_specs=(
            P("dp", "tensor"),
            P("dp", "tensor"),
            P("dp", None),
            P(),
            P("tensor", None),
            P(("tensor", "dp"), None),
            P(("tensor", "dp"), None),
            P(("tensor", "dp"), None),
        ),
        out_specs=(
            P(("tensor", "dp"), None),
            P(("tensor", "dp"), None),
            P(("tensor", "dp"), None),
            P(("tensor", "dp"), None),
            P(("dp", "tensor"), None),
        ),
        check_vma=False,
    )
```

```python
import math

import jax
import jax.numpy as jnp
import numpy as np
from jax import lax
from jax.experimental import pallas as pl
from jax.experimental.pallas import tpu as pltpu
from jax.sharding import PartitionSpec as P

BLOCK = 256


CLIP_LEVEL = 127.0
LEARN_RATE = 0.005
BETA_ONE = 0.9
BETA_TWO = 0.95
WEIGHT_DECAY = 0.1
EPSILON = 1e-08
FIRST_BIAS = 1.0 - (0.9**50) ** 2
SECOND_BIAS = 1.0 - (0.95**50) ** 2
LEVELS = (16.0, 32.0, 64.0, 128.0)
CHUNKS = 4
GROUPS = 4
ADAM_STEPS = 2
FORWARD_STEPS = 2
ORDER = (
    "rot",
    "tu0",
    "g10",
    "tu3",
    "g11",
    "tu2",
    "g12",
    "ay0",
    "g13",
    "ay1",
    "ad0",
    "tu1",
    "ay2",
    "ad1",
    "g20",
    "ay3",
    "ad2",
    "g21",
    "sc0",
    "ad3",
    "g22",
    "sc1",
    "sx0",
    "g23",
    "sc2",
    "sx1",
    "sn0",
    "sc3",
    "sx2",
    "sn1",
    "sx3",
    "sn2",
    "sn3",
)
COST = {"ro": 300000000, "st": 25000000000, "ay": 300000000, "g1": 300000000, "ad": 300000000, "tu": 300000000, "g2": 300000000, "sc": 300000000, "sx": 300000000, "sn": 300000000}
VMEM_BYTES = 28 * 1024 * 1024


def hadamard(block_size):
    positions = np.arange(block_size)
    common_bits = positions[:, None] & positions[None, :]
    parity = np.zeros((block_size, block_size), np.int32)
    for bit_shift in range(block_size.bit_length() - 1):
        parity += (common_bits >> bit_shift) & 1
    return ((1 - 2 * (parity & 1)) / math.sqrt(block_size)).astype(np.float32)


def dot(a, b):
    return lax.dot_general(a, b, (((1,), (0,)), ((), ())), preferred_element_type=jnp.float32)


def block_spec(shape, index_map):
    return pl.BlockSpec(shape, index_map)


def whole(shape):
    return pl.BlockSpec(shape, lambda i, p: (0,) * len(shape))


class Chain:
    def __init__(self, place):
        self.place = place
        self.held = []

    def note(self, value):
        self.held.append(value)

    def __call__(self, name, body, grid, in_specs, out_specs, out_shape, scratch, args, aliases=None, token=0):
        held = self.held
        count, extra = len(args), len(held)

        def wrapped(place_ref, *refs):
            body(place_ref, *refs[:count], *refs[count + extra :])

        outs = pl.pallas_call(
            wrapped,
            grid_spec=pltpu.PrefetchScalarGridSpec(
                num_scalar_prefetch=1,
                grid=grid,
                in_specs=list(in_specs) + [pl.BlockSpec(memory_space=pl.ANY)] * extra,
                out_specs=out_specs,
                scratch_shapes=scratch,
            ),
            out_shape=out_shape,
            input_output_aliases=aliases or {},
            compiler_params=pltpu.CompilerParams(vmem_limit_bytes=VMEM_BYTES),
            cost_estimate=pl.CostEstimate(flops=COST[name[:2]], bytes_accessed=1000, transcendentals=0),
        )(self.place, *args, *held)
        self.held = [outs[token]]
        return outs


def rotate(chain, out_grad, flips, matrix):
    rows, width = out_grad.shape
    step = width // CHUNKS
    piece = step // 4
    per_group = CHUNKS // GROUPS

    def body(place_ref, grad_ref, flips_ref, matrix_ref, out_ref, *own_refs):
        position = place_ref[0]
        for block in range(step // BLOCK):
            columns = slice(block * BLOCK, (block + 1) * BLOCK)
            signed = grad_ref[:, columns] * flips_ref[block]
            out_ref[:, columns] = dot(signed, matrix_ref[...]).astype(jnp.bfloat16)
        for chunk in range(CHUNKS):

            @pl.when(pl.program_id(0) == chunk)
            def _():
                start = (chunk % per_group) * piece
                own = out_ref[:, pl.ds(pl.multiple_of(position * piece, BLOCK), piece)]
                own_refs[chunk // per_group][:, start : start + piece] = own

    return chain(
        "rot",
        body,
        (CHUNKS,),
        [
            block_spec((rows, step), lambda b, p: (0, b)),
            block_spec((step // BLOCK, 1, BLOCK), lambda b, p: (b, 0, 0)),
            whole((BLOCK, BLOCK)),
        ],
        [block_spec((rows, step), lambda b, p: (0, b))] + [whole((rows, per_group * piece))] * GROUPS,
        [jax.ShapeDtypeStruct((rows, width), jnp.bfloat16)]
        + [jax.ShapeDtypeStruct((rows, per_group * piece), jnp.bfloat16)] * GROUPS,
        [],
        (out_grad, flips.reshape(width // BLOCK, 1, BLOCK), matrix),
    )


def coded_sum(chain, chunk, hidden_parts, rotated, pieces, scales):
    units, tokens = hidden_parts[0].shape
    rows = units // 4
    width = rotated.shape[1] // CHUNKS
    piece = width // 4
    block_count = scales.shape[1]

    def body(place_ref, h0, h1, own_ref, u_ref, cu_ref, v_ref, cv_ref, scales_ref, keep_ref, send_ref, acc_ref):
        position, y = place_ref[0], place_ref[1]
        mine = pl.ds(pl.multiple_of(y * rows, 8), rows)
        theirs = pl.ds(pl.multiple_of((1 - y) * rows, 8), rows)
        lane = lax.broadcasted_iota(jnp.int32, (2 * rows, block_count), 1)
        all_scales = scales_ref[...]
        for j, ref in enumerate((u_ref, cu_ref, v_ref, cv_ref)):
            quarter = jnp.bitwise_xor(position, j)
            for part in range(piece // BLOCK):
                column = pl.multiple_of(quarter * piece + part * BLOCK, BLOCK)
                columns = pl.ds(column, BLOCK)
                block = chunk * (width // BLOCK) + quarter * (piece // BLOCK) + part
                scale = jnp.sum(jnp.where(lane == block, all_scales, 0.0), axis=1, keepdims=True)

                def coded(hidden, values):
                    product = dot(hidden, values) * scale
                    return jnp.clip(product, -CLIP_LEVEL, CLIP_LEVEL).astype(jnp.bfloat16).astype(jnp.float32)

                acc_ref[...] = coded(h0[...], own_ref[:, columns]) + coded(
                    h1[...], ref[:, part * BLOCK : (part + 1) * BLOCK]
                )
                keep_ref[0, :, columns] = acc_ref[mine, :].astype(jnp.bfloat16)
                send_ref[0, :, columns] = acc_ref[theirs, :].astype(jnp.bfloat16)

    out = jax.ShapeDtypeStruct((2, rows, width), jnp.bfloat16)
    part_spec = block_spec((tokens, piece), lambda i, p: (0, chunk % (CHUNKS // GROUPS)))
    return chain(
        f"g1{chunk}",
        body,
        (2,),
        [block_spec((2 * rows, tokens), lambda i, p: (i, 0))] * 2
        + [block_spec((tokens, width), lambda i, p: (0, chunk))]
        + [part_spec] * 4
        + [block_spec((2 * rows, block_count), lambda i, p: (i, 0))],
        [block_spec((1, rows, width), lambda i, p: (i, 0, 0))] * 2,
        [out, out],
        [pltpu.VMEM((2 * rows, BLOCK), jnp.float32)],
        (*hidden_parts, rotated, *pieces, scales),
    )


def adam(chain, chunk, kept, received, shard_scales, flips, matrix, master, one, two, previous):
    rows, width = kept.shape
    model_width = master.shape[1]
    block_count = shard_scales.shape[1]
    step = width // ADAM_STEPS
    parts = step // BLOCK
    chained = previous is not None

    def body(place_ref, kept_ref, received_ref, scales_ref, flips_ref, matrix_ref, master_ref, one_ref, two_ref, *rest):
        grad_out, master_out, one_out, two_out, weight_out = rest[-5:]
        lane = lax.broadcasted_iota(jnp.int32, (rows, block_count), 1)
        all_scales = scales_ref[...]
        for part in range(parts):
            block = (chunk * ADAM_STEPS + pl.program_id(0)) * parts + part
            columns = slice(part * BLOCK, (part + 1) * BLOCK)
            scale = jnp.sum(jnp.where(lane == block, all_scales, 0.0), axis=1, keepdims=True)
            decoded = dot(kept_ref[:, columns], matrix_ref[...]) + dot(received_ref[:, columns], matrix_ref[...])
            gradient = decoded / scale * flips_ref[part]
            new_one = BETA_ONE * one_ref[:, columns] + (1.0 - BETA_ONE) * gradient
            new_two = BETA_TWO * two_ref[:, columns] + (1.0 - BETA_TWO) * gradient * gradient
            update = new_one / FIRST_BIAS / (jnp.sqrt(new_two / SECOND_BIAS) + EPSILON)
            old = master_ref[:, columns]
            new_master = old - LEARN_RATE * (update + WEIGHT_DECAY * old)
            grad_out[:, columns] = gradient
            master_out[:, columns] = new_master
            one_out[:, columns] = new_one
            two_out[:, columns] = new_two
            weight_out[:, columns] = new_master.astype(jnp.bfloat16)

    local = block_spec((rows, step), lambda j, p: (0, j))
    placed = block_spec((rows, step), lambda j, p: (0, chunk * ADAM_STEPS + j))
    state = jax.ShapeDtypeStruct((rows, model_width), jnp.float32)
    return chain(
        f"ad{chunk}",
        body,
        (ADAM_STEPS,),
        [
            local,
            local,
            whole((rows, block_count)),
            block_spec((parts, 1, BLOCK), lambda j, p: (chunk * ADAM_STEPS + j, 0, 0)),
            whole((BLOCK, BLOCK)),
            placed,
            placed,
            placed,
        ]
        + ([pl.BlockSpec(memory_space=pl.ANY)] * 4 if chained else []),
        [placed] * 4 + [local],
        [state] * 4 + [jax.ShapeDtypeStruct((rows, width), jnp.bfloat16)],
        [],
        (
            kept,
            received,
            shard_scales,
            flips.astype(jnp.float32).reshape(block_count, 1, BLOCK),
            matrix,
            *(pltpu.with_memory_space_constraint(value, pltpu.HBM) for value in (master, one, two)),
            *(previous if chained else ()),
        ),
        {9 + i: i for i in range(4)} if chained else None,
        token=4,
    )


def forward(chain, name, inputs, weight, other):
    tokens, units = inputs[0].shape
    rows, width = weight.shape
    quarter = tokens // 4
    step = width // FORWARD_STEPS

    def body(place_ref, n0, n1, n2, n3, weight_ref, other_ref, o0, o1, o2, o3, acc_ref, joined_ref):
        position, y = place_ref[0], place_ref[1]
        joined_ref[pl.ds(pl.multiple_of(y * rows, 8), rows), :] = weight_ref[...].astype(jnp.float32)
        joined_ref[pl.ds(pl.multiple_of((1 - y) * rows, 8), rows), :] = other_ref[...].astype(jnp.float32)
        joined = joined_ref[...].astype(jnp.bfloat16)
        for k, ref in enumerate((n0, n2, n1, n3)):
            acc_ref[...] = dot(ref[...], joined).astype(jnp.bfloat16)
            for i, out_ref in enumerate((o0, o1, o2, o3)):
                start = jnp.bitwise_xor(position, i) * quarter
                out_ref[k] = acc_ref[pl.ds(pl.multiple_of(start, quarter), quarter), :]

    return chain(
        name,
        body,
        (FORWARD_STEPS,),
        [whole((tokens, units))] * 4 + [block_spec((rows, step), lambda j, p: (0, j))] * 2,
        [block_spec((4, quarter, step), lambda j, p: (0, 0, j))] * 4,
        [jax.ShapeDtypeStruct((4, quarter, width), jnp.bfloat16)] * 4,
        [pltpu.VMEM((tokens, step), jnp.bfloat16), pltpu.VMEM((units, step), jnp.float32)],
        (*inputs, weight, other),
    )


def add(a, b):
    return (a.astype(jnp.float32) + b.astype(jnp.float32)).astype(jnp.bfloat16)


def on_device(
    hidden, next_hidden, out_grad, sign_bits, scale_index, master, moment_one, moment_two
):
    dp_size = lax.axis_size("dp")
    tensor_size = lax.axis_size("tensor")
    tokens = hidden.shape[0]
    shard_rows = master.shape[0]
    block_count = sign_bits.shape[0]
    replica = lax.axis_index("dp")
    group = lax.axis_index("tensor")
    z, y = replica // 2, replica % 2
    far_side = replica // 4
    place = jnp.stack([group, y, far_side]).astype(jnp.int32)
    matrix = jnp.asarray(hadamard(BLOCK)).astype(jnp.bfloat16)
    flips = (1 - 2 * sign_bits).astype(jnp.bfloat16)

    def over_dp(value, bits):
        return lax.ppermute(value, "dp", [(i, i ^ bits) for i in range(dp_size)])

    def over_tensor(value, bits):
        return lax.ppermute(value, "tensor", [(i, i ^ bits) for i in range(tensor_size)])

    units = 2 * shard_rows
    near_z = z % 2
    by_pair = hidden.T.reshape(2, 2, units, tokens)

    def pair_rows(values, k):
        picked = lax.dynamic_index_in_dim(values, near_z ^ k, 1, keepdims=False)
        return picked.reshape(2 * units, picked.shape[-1])

    hidden_parts = [pair_rows(by_pair, 0), over_dp(pair_rows(by_pair, 1), 2)]
    chain = Chain(place)
    rotated, *own_pieces = rotate(chain, out_grad, flips, matrix)

    level_table = jnp.array(LEVELS, jnp.float32)
    matches = (scale_index[:, :, None] == jnp.arange(4, dtype=jnp.int32)).astype(jnp.float32)
    all_scales = jnp.sum(matches * level_table, axis=-1) * math.sqrt(dp_size)
    scales = pair_rows(all_scales.reshape(2, 2, units, block_count), 0)
    shard_scales = lax.dynamic_slice_in_dim(scales, (2 * far_side + y) * shard_rows, shard_rows, 0)

    next_t = next_hidden.T
    inputs = [lax.dynamic_slice_in_dim(next_t, (z ^ k) * units, units, 0) for k in range(4)]
    inputs = [inputs[0]] + [over_dp(inputs[k], 2 * k) for k in range(1, 4)]

    state = None
    pieces, kept, halves, arriving, weights, partials, sums, nears, outs = ({} for _ in range(9))
    turned_inputs = {}

    def gather(k):
        u = over_dp(own_pieces[k], 2)
        v = over_tensor(u, 2)
        pieces[k] = (u, over_tensor(u, 1), v, over_tensor(v, 1))

    def first(k):
        kept[k], sent = coded_sum(chain, k, hidden_parts, rotated, pieces[k // (CHUNKS // GROUPS)], scales)
        halves[k] = over_dp(sent, 1)

    def join_rows(k):
        def side(value, index):
            return lax.dynamic_index_in_dim(value, index, 0, keepdims=False)

        go = add(side(kept[k], 1 - far_side), side(halves[k], 1 - far_side))
        kept[k] = add(side(kept[k], far_side), side(halves[k], far_side))
        arriving[k] = over_dp(go, 4)
        chain.note(go)

    def update(k):
        nonlocal state
        *state, weight = adam(
            chain, k, kept[k], arriving[k], shard_scales, flips, matrix, master, moment_one, moment_two, state
        )
        weights[k] = (weight, over_dp(weight, 1))

    def turn(k):
        turned_inputs[k] = inputs[k].T
        chain.note(inputs[k])

    def second(k):
        stay, near, go, far = forward(chain, f"g2{k}", [turned_inputs[i] for i in range(4)], *weights[k])
        partials[k] = (stay, go, over_tensor(near, 1), over_tensor(far, 1))

    def sum_cores(k):
        stay, go, near, far = partials[k]
        go = add(go, far)
        sums[k] = (add(stay, near), over_tensor(go, 2))
        chain.note(go)

    def sum_chips(k):
        stay, more = sums[k]
        go = add(stay[2:], more[2:])
        nears[k] = (add(stay[:2], more[:2]), over_dp(go, 2))
        chain.note(go)

    def sum_near(k):
        stay, more = nears[k]
        go = add(stay[1], more[1])
        outs[k] = (add(stay[0], more[0]), over_dp(go, 4))
        chain.note(go)

    steps = {"tu": turn, "ay": join_rows, "g1": first, "ad": update, "g2": second, "sc": sum_cores, "sx": sum_chips, "sn": sum_near}
    for group_index in range(GROUPS):
        gather(group_index)
    for name in ORDER[1:]:
        steps[name[:2]](int(name[2:]))
    next_out = jnp.concatenate([add(*outs[k]) for k in range(CHUNKS)], axis=1)
    gradient, new_master, new_one, new_two = state
    return (gradient, new_master, new_one, new_two, next_out)


def general(
    hidden, next_hidden, out_grad, sign_bits, scale_index, master, moment_one, moment_two
):
    dp_size = lax.axis_size("dp")
    tok_rows = hidden.shape[0]
    model_width = out_grad.shape[1]
    block_count = sign_bits.shape[0]
    shard_rows = master.shape[0]
    matrix = jnp.asarray(hadamard(BLOCK))
    sign_flips = (1 - 2 * sign_bits).astype(jnp.float32)
    signed = out_grad.reshape(tok_rows, block_count, BLOCK) * sign_flips.astype(jnp.bfloat16)
    rotated = jnp.einsum(
        "tbj,jk->tbk", signed, matrix.astype(jnp.bfloat16), preferred_element_type=jnp.float32
    )
    rotated = rotated.astype(jnp.bfloat16).reshape(tok_rows, model_width)
    level_table = jnp.array(LEVELS, jnp.float32)
    matches = (scale_index[:, :, None] == jnp.arange(4, dtype=jnp.int32)).astype(jnp.float32)
    scales = jnp.sum(matches * level_table, axis=-1) * math.sqrt(dp_size)
    product = lax.dot_general(
        hidden, rotated, (((0,), (0,)), ((), ())), preferred_element_type=jnp.float32
    )
    scaled = product.reshape(dp_size * shard_rows, block_count, BLOCK) * scales[:, :, None]
    summed = lax.psum_scatter(
        jnp.clip(scaled, -CLIP_LEVEL, CLIP_LEVEL)
        .reshape(dp_size * shard_rows, model_width)
        .astype(jnp.bfloat16),
        "dp",
        scatter_dimension=0,
        tiled=True,
    ).astype(jnp.float32)
    shard_scales = lax.dynamic_slice_in_dim(
        scales, lax.axis_index("dp") * shard_rows, shard_rows, 0
    )
    unscaled = summed.reshape(shard_rows, block_count, BLOCK) / shard_scales[:, :, None]
    decoded = jnp.einsum("rbj,jk->rbk", unscaled, matrix, precision=lax.Precision.HIGHEST)
    gradient = (decoded * sign_flips).reshape(shard_rows, model_width)
    new_one = BETA_ONE * moment_one + (1.0 - BETA_ONE) * gradient
    new_two = BETA_TWO * moment_two + (1.0 - BETA_TWO) * gradient * gradient
    update = new_one / FIRST_BIAS / (jnp.sqrt(new_two / SECOND_BIAS) + EPSILON)
    new_master = master - LEARN_RATE * (update + WEIGHT_DECAY * master)
    partial_value = jnp.dot(
        next_hidden,
        lax.all_gather(new_master.astype(jnp.bfloat16), "dp", axis=0, tiled=True),
        preferred_element_type=jnp.float32,
    )
    next_out = lax.psum_scatter(
        partial_value.astype(jnp.bfloat16), "tensor", scatter_dimension=0, tiled=True
    )
    return (gradient, new_master, new_one, new_two, next_out)


def solution(mesh):
    grouped = mesh.shape["dp"] == 8 and mesh.shape["tensor"] == 4
    return jax.shard_map(
        on_device if grouped else general,
        mesh=mesh,
        in_specs=(
            P("dp", "tensor"),
            P("dp", "tensor"),
            P("dp", None),
            P(),
            P("tensor", None),
            P(("tensor", "dp"), None),
            P(("tensor", "dp"), None),
            P(("tensor", "dp"), None),
        ),
        out_specs=(
            P(("tensor", "dp"), None),
            P(("tensor", "dp"), None),
            P(("tensor", "dp"), None),
            P(("tensor", "dp"), None),
            P(("dp", "tensor"), None),
        ),
        check_vma=False,
    )
```

```python
import math

import jax
import jax.numpy as jnp
import numpy as np
from jax import lax
from jax.experimental import pallas as pl
from jax.experimental.pallas import tpu as pltpu
from jax.sharding import PartitionSpec as P

BLOCK = 256


CLIP_LEVEL = 127.0
LEARN_RATE = 0.005
BETA_ONE = 0.9
BETA_TWO = 0.95
WEIGHT_DECAY = 0.1
EPSILON = 1e-08
FIRST_BIAS = 1.0 - (0.9**50) ** 2
SECOND_BIAS = 1.0 - (0.95**50) ** 2
LEVELS = (16.0, 32.0, 64.0, 128.0)
CHUNKS = 4
GROUPS = 4
ADAM_STEPS = 2
FORWARD_STEPS = 2
ORDER = (
    "rot",
    "g10",
    "g11",
    "tu2",
    "g12",
    "ay0",
    "g13",
    "ay1",
    "ad0",
    "tu1",
    "ay2",
    "ad1",
    "g20",
    "ay3",
    "ad2",
    "g21",
    "sc0",
    "ad3",
    "g22",
    "sc1",
    "sx0",
    "g23",
    "sc2",
    "sx1",
    "sn0",
    "sc3",
    "sx2",
    "sn1",
    "sx3",
    "sn2",
    "sn3",
)
COST = {"ro": 300000000, "st": 25000000000, "ay": 300000000, "g1": 300000000, "ad": 300000000, "tu": 300000000, "g2": 300000000, "sc": 300000000, "sx": 300000000, "sn": 300000000}
VMEM_BYTES = 28 * 1024 * 1024


def hadamard(block_size):
    positions = np.arange(block_size)
    common_bits = positions[:, None] & positions[None, :]
    parity = np.zeros((block_size, block_size), np.int32)
    for bit_shift in range(block_size.bit_length() - 1):
        parity += (common_bits >> bit_shift) & 1
    return ((1 - 2 * (parity & 1)) / math.sqrt(block_size)).astype(np.float32)


def dot(a, b):
    return lax.dot_general(a, b, (((1,), (0,)), ((), ())), preferred_element_type=jnp.float32)


def block_spec(shape, index_map):
    return pl.BlockSpec(shape, index_map)


def whole(shape):
    return pl.BlockSpec(shape, lambda i, p: (0,) * len(shape))


class Chain:
    def __init__(self, place):
        self.place = place
        self.held = []

    def note(self, value):
        self.held.append(value)

    def __call__(self, name, body, grid, in_specs, out_specs, out_shape, scratch, args, aliases=None, token=0):
        held = self.held
        count, extra = len(args), len(held)

        def wrapped(place_ref, *refs):
            body(place_ref, *refs[:count], *refs[count + extra :])

        outs = pl.pallas_call(
            wrapped,
            grid_spec=pltpu.PrefetchScalarGridSpec(
                num_scalar_prefetch=1,
                grid=grid,
                in_specs=list(in_specs) + [pl.BlockSpec(memory_space=pl.ANY)] * extra,
                out_specs=out_specs,
                scratch_shapes=scratch,
            ),
            out_shape=out_shape,
            input_output_aliases=aliases or {},
            compiler_params=pltpu.CompilerParams(vmem_limit_bytes=VMEM_BYTES),
            cost_estimate=pl.CostEstimate(flops=COST[name[:2]], bytes_accessed=1000, transcendentals=0),
        )(self.place, *args, *held)
        self.held = [outs[token]]
        return outs


def rotate(chain, out_grad, flips, matrix):
    rows, width = out_grad.shape
    step = width // CHUNKS
    piece = step // 4
    per_group = CHUNKS // GROUPS

    def body(place_ref, grad_ref, flips_ref, matrix_ref, out_ref, *own_refs):
        position = place_ref[0]
        for block in range(step // BLOCK):
            columns = slice(block * BLOCK, (block + 1) * BLOCK)
            signed = grad_ref[:, columns] * flips_ref[block]
            out_ref[:, columns] = dot(signed, matrix_ref[...]).astype(jnp.bfloat16)
        for chunk in range(CHUNKS):

            @pl.when(pl.program_id(0) == chunk)
            def _():
                start = (chunk % per_group) * piece
                own = out_ref[:, pl.ds(pl.multiple_of(position * piece, BLOCK), piece)]
                own_refs[chunk // per_group][:, start : start + piece] = own

    return chain(
        "rot",
        body,
        (CHUNKS,),
        [
            block_spec((rows, step), lambda b, p: (0, b)),
            block_spec((step // BLOCK, 1, BLOCK), lambda b, p: (b, 0, 0)),
            whole((BLOCK, BLOCK)),
        ],
        [block_spec((rows, step), lambda b, p: (0, b))] + [whole((rows, per_group * piece))] * GROUPS,
        [jax.ShapeDtypeStruct((rows, width), jnp.bfloat16)]
        + [jax.ShapeDtypeStruct((rows, per_group * piece), jnp.bfloat16)] * GROUPS,
        [],
        (out_grad, flips.reshape(width // BLOCK, 1, BLOCK), matrix),
    )


def coded_sum(chain, chunk, hidden_parts, rotated, pieces, scales):
    units, tokens = hidden_parts[0].shape
    rows = units // 2
    width = rotated.shape[1] // CHUNKS
    piece = width // 4
    block_count = scales.shape[1]

    def body(place_ref, h0, h1, g0, g1, own_ref, u_ref, cu_ref, v_ref, cv_ref, scales_ref, keep_ref, send_ref, acc_ref):
        position, y = place_ref[0], place_ref[1]
        mine = pl.ds(pl.multiple_of(y * rows, 8), rows)
        theirs = pl.ds(pl.multiple_of((1 - y) * rows, 8), rows)
        lane = lax.broadcasted_iota(jnp.int32, (2 * rows, block_count), 1)
        all_scales = scales_ref[...]
        for j, ref in enumerate((u_ref, cu_ref, v_ref, cv_ref)):
            quarter = jnp.bitwise_xor(position, j)
            for part in range(piece // BLOCK):
                column = pl.multiple_of(quarter * piece + part * BLOCK, BLOCK)
                columns = pl.ds(column, BLOCK)
                block = chunk * (width // BLOCK) + quarter * (piece // BLOCK) + part
                scale = jnp.sum(jnp.where(lane == block, all_scales, 0.0), axis=1, keepdims=True)

                def coded(hidden, values):
                    product = dot(hidden, values) * scale
                    return jnp.clip(product, -CLIP_LEVEL, CLIP_LEVEL).astype(jnp.bfloat16).astype(jnp.float32)

                values, other = own_ref[:, columns], ref[:, part * BLOCK : (part + 1) * BLOCK]

                @pl.when(pl.program_id(0) == 0)
                def _():
                    acc_ref[...] = coded(h0[...], values) + coded(g0[...], other)

                @pl.when(pl.program_id(0) == 1)
                def _():
                    acc_ref[...] = coded(h1[...], values) + coded(g1[...], other)

                keep_ref[0, :, columns] = acc_ref[mine, :].astype(jnp.bfloat16)
                send_ref[0, :, columns] = acc_ref[theirs, :].astype(jnp.bfloat16)

    out = jax.ShapeDtypeStruct((2, rows, width), jnp.bfloat16)
    part_spec = block_spec((tokens, piece), lambda i, p: (0, chunk % (CHUNKS // GROUPS)))
    return chain(
        f"g1{chunk}",
        body,
        (2,),
        [whole((units, tokens))] * 4
        + [block_spec((tokens, width), lambda i, p: (0, chunk))]
        + [part_spec] * 4
        + [block_spec((2 * rows, block_count), lambda i, p: (i, 0))],
        [block_spec((1, rows, width), lambda i, p: (jnp.bitwise_xor(i, p[2]), 0, 0))] * 2,
        [out, out],
        [pltpu.VMEM((2 * rows, BLOCK), jnp.float32)],
        (*hidden_parts, rotated, *pieces, scales),
    )


def adam(chain, chunk, kept, received, shard_scales, flips, matrix, master, one, two, previous):
    rows, width = kept.shape
    model_width = master.shape[1]
    block_count = shard_scales.shape[1]
    step = width // ADAM_STEPS
    parts = step // BLOCK
    chained = previous is not None

    def body(place_ref, kept_ref, received_ref, scales_ref, flips_ref, matrix_ref, master_ref, one_ref, two_ref, *rest):
        grad_out, master_out, one_out, two_out, weight_out = rest[-5:]
        lane = lax.broadcasted_iota(jnp.int32, (rows, block_count), 1)
        all_scales = scales_ref[...]
        for part in range(parts):
            block = (chunk * ADAM_STEPS + pl.program_id(0)) * parts + part
            columns = slice(part * BLOCK, (part + 1) * BLOCK)
            scale = jnp.sum(jnp.where(lane == block, all_scales, 0.0), axis=1, keepdims=True)
            decoded = dot(kept_ref[:, columns], matrix_ref[...]) + dot(received_ref[:, columns], matrix_ref[...])
            gradient = decoded / scale * flips_ref[part]
            new_one = BETA_ONE * one_ref[:, columns] + (1.0 - BETA_ONE) * gradient
            new_two = BETA_TWO * two_ref[:, columns] + (1.0 - BETA_TWO) * gradient * gradient
            update = new_one / FIRST_BIAS / (jnp.sqrt(new_two / SECOND_BIAS) + EPSILON)
            old = master_ref[:, columns]
            new_master = old - LEARN_RATE * (update + WEIGHT_DECAY * old)
            grad_out[:, columns] = gradient
            master_out[:, columns] = new_master
            one_out[:, columns] = new_one
            two_out[:, columns] = new_two
            weight_out[:, columns] = new_master.astype(jnp.bfloat16)

    local = block_spec((rows, step), lambda j, p: (0, j))
    placed = block_spec((rows, step), lambda j, p: (0, chunk * ADAM_STEPS + j))
    state = jax.ShapeDtypeStruct((rows, model_width), jnp.float32)
    return chain(
        f"ad{chunk}",
        body,
        (ADAM_STEPS,),
        [
            local,
            local,
            whole((rows, block_count)),
            block_spec((parts, 1, BLOCK), lambda j, p: (chunk * ADAM_STEPS + j, 0, 0)),
            whole((BLOCK, BLOCK)),
            placed,
            placed,
            placed,
        ]
        + ([pl.BlockSpec(memory_space=pl.ANY)] * 4 if chained else []),
        [placed] * 4 + [local],
        [state] * 4 + [jax.ShapeDtypeStruct((rows, width), jnp.bfloat16)],
        [],
        (
            kept,
            received,
            shard_scales,
            flips.astype(jnp.float32).reshape(block_count, 1, BLOCK),
            matrix,
            *(pltpu.with_memory_space_constraint(value, pltpu.HBM) for value in (master, one, two)),
            *(previous if chained else ()),
        ),
        {9 + i: i for i in range(4)} if chained else None,
        token=4,
    )


def forward(chain, name, inputs, weight, other):
    tokens, units = inputs[0].shape
    rows, width = weight.shape
    quarter = tokens // 4
    step = width // FORWARD_STEPS

    def body(place_ref, n0, n1, n2, n3, weight_ref, other_ref, o0, o1, o2, o3, acc_ref, joined_ref):
        position, y = place_ref[0], place_ref[1]
        joined_ref[pl.ds(pl.multiple_of(y * rows, 8), rows), :] = weight_ref[...].astype(jnp.float32)
        joined_ref[pl.ds(pl.multiple_of((1 - y) * rows, 8), rows), :] = other_ref[...].astype(jnp.float32)
        joined = joined_ref[...].astype(jnp.bfloat16)
        for k, ref in enumerate((n0, n2, n1, n3)):
            acc_ref[...] = dot(ref[...], joined).astype(jnp.bfloat16)
            for i, out_ref in enumerate((o0, o1, o2, o3)):
                start = jnp.bitwise_xor(position, i) * quarter
                out_ref[k] = acc_ref[pl.ds(pl.multiple_of(start, quarter), quarter), :]

    return chain(
        name,
        body,
        (FORWARD_STEPS,),
        [whole((tokens, units))] * 4 + [block_spec((rows, step), lambda j, p: (0, j))] * 2,
        [block_spec((4, quarter, step), lambda j, p: (0, 0, j))] * 4,
        [jax.ShapeDtypeStruct((4, quarter, width), jnp.bfloat16)] * 4,
        [pltpu.VMEM((tokens, step), jnp.bfloat16), pltpu.VMEM((units, step), jnp.float32)],
        (*inputs, weight, other),
    )


def add(a, b):
    return (a.astype(jnp.float32) + b.astype(jnp.float32)).astype(jnp.bfloat16)


def on_device(
    hidden, next_hidden, out_grad, sign_bits, scale_index, master, moment_one, moment_two
):
    dp_size = lax.axis_size("dp")
    tensor_size = lax.axis_size("tensor")
    tokens = hidden.shape[0]
    shard_rows = master.shape[0]
    block_count = sign_bits.shape[0]
    replica = lax.axis_index("dp")
    group = lax.axis_index("tensor")
    z, y = replica // 2, replica % 2
    far_side = replica // 4
    place = jnp.stack([group, y, far_side]).astype(jnp.int32)
    matrix = jnp.asarray(hadamard(BLOCK)).astype(jnp.bfloat16)
    flips = (1 - 2 * sign_bits).astype(jnp.bfloat16)

    def over_dp(value, bits):
        return lax.ppermute(value, "dp", [(i, i ^ bits) for i in range(dp_size)])

    def over_tensor(value, bits):
        return lax.ppermute(value, "tensor", [(i, i ^ bits) for i in range(tensor_size)])

    units = 2 * shard_rows
    near_z = z % 2
    by_pair = hidden.T.reshape(2, 2, units, tokens)

    def pair_rows(values, k):
        picked = lax.dynamic_index_in_dim(values, near_z ^ k, 1, keepdims=False)
        return picked.reshape(2 * units, picked.shape[-1])

    hidden_parts = [lax.dynamic_index_in_dim(half, near_z, 0, keepdims=False) for half in by_pair]
    hidden_parts += [
        over_dp(lax.dynamic_index_in_dim(half, 1 - near_z, 0, keepdims=False), 2) for half in by_pair
    ]
    chain = Chain(place)
    rotated, *own_pieces = rotate(chain, out_grad, flips, matrix)

    level_table = jnp.array(LEVELS, jnp.float32)
    matches = (scale_index[:, :, None] == jnp.arange(4, dtype=jnp.int32)).astype(jnp.float32)
    all_scales = jnp.sum(matches * level_table, axis=-1) * math.sqrt(dp_size)
    scales = pair_rows(all_scales.reshape(2, 2, units, block_count), 0)
    shard_scales = lax.dynamic_slice_in_dim(scales, (2 * far_side + y) * shard_rows, shard_rows, 0)

    by_z = next_hidden.T.reshape(4, units, tokens)

    def for_z(k):
        return lax.dynamic_index_in_dim(by_z, z ^ k, 0, keepdims=False)

    across = over_dp(jnp.stack([for_z(2), for_z(3)]), 4)
    beside = over_dp(jnp.stack([for_z(1), across[1]]), 2)
    inputs = [for_z(0), beside[0], across[0], beside[1]]

    state = None
    pieces, kept, halves, arriving, weights, partials, sums, nears, outs = ({} for _ in range(9))
    turned_inputs = {k: value.T for k, value in enumerate(inputs)}

    def gather(k):
        u = over_dp(own_pieces[k], 2)
        v = over_tensor(u, 2)
        pieces[k] = (u, over_tensor(u, 1), v, over_tensor(v, 1))

    def first(k):
        kept[k], sent = coded_sum(chain, k, hidden_parts, rotated, pieces[k // (CHUNKS // GROUPS)], scales)
        halves[k] = over_dp(sent, 1)

    def join_rows(k):
        go = add(kept[k][1], halves[k][1])
        kept[k] = add(kept[k][0], halves[k][0])
        arriving[k] = over_dp(go, 4)
        chain.note(go)

    def update(k):
        nonlocal state
        *state, weight = adam(
            chain, k, kept[k], arriving[k], shard_scales, flips, matrix, master, moment_one, moment_two, state
        )
        weights[k] = (weight, over_dp(weight, 1))

    def turn(k):
        chain.note((inputs[0], beside, across, beside)[k])

    def second(k):
        stay, near, go, far = forward(chain, f"g2{k}", [turned_inputs[i] for i in range(4)], *weights[k])
        partials[k] = (stay, go, over_tensor(near, 1), over_tensor(far, 1))

    def sum_cores(k):
        stay, go, near, far = partials[k]
        go = add(go, far)
        sums[k] = (add(stay, near), over_tensor(go, 2))
        chain.note(go)

    def sum_chips(k):
        stay, more = sums[k]
        go = add(stay[2:], more[2:])
        nears[k] = (add(stay[:2], more[:2]), over_dp(go, 2))
        chain.note(go)

    def sum_near(k):
        stay, more = nears[k]
        go = add(stay[1], more[1])
        outs[k] = (add(stay[0], more[0]), over_dp(go, 4))
        chain.note(go)

    steps = {"tu": turn, "ay": join_rows, "g1": first, "ad": update, "g2": second, "sc": sum_cores, "sx": sum_chips, "sn": sum_near}
    for group_index in range(GROUPS):
        gather(group_index)
    for name in ORDER[1:]:
        steps[name[:2]](int(name[2:]))
    next_out = jnp.concatenate([add(*outs[k]) for k in range(CHUNKS)], axis=1)
    gradient, new_master, new_one, new_two = state
    return (gradient, new_master, new_one, new_two, next_out)


def general(
    hidden, next_hidden, out_grad, sign_bits, scale_index, master, moment_one, moment_two
):
    dp_size = lax.axis_size("dp")
    tok_rows = hidden.shape[0]
    model_width = out_grad.shape[1]
    block_count = sign_bits.shape[0]
    shard_rows = master.shape[0]
    matrix = jnp.asarray(hadamard(BLOCK))
    sign_flips = (1 - 2 * sign_bits).astype(jnp.float32)
    signed = out_grad.reshape(tok_rows, block_count, BLOCK) * sign_flips.astype(jnp.bfloat16)
    rotated = jnp.einsum(
        "tbj,jk->tbk", signed, matrix.astype(jnp.bfloat16), preferred_element_type=jnp.float32
    )
    rotated = rotated.astype(jnp.bfloat16).reshape(tok_rows, model_width)
    level_table = jnp.array(LEVELS, jnp.float32)
    matches = (scale_index[:, :, None] == jnp.arange(4, dtype=jnp.int32)).astype(jnp.float32)
    scales = jnp.sum(matches * level_table, axis=-1) * math.sqrt(dp_size)
    product = lax.dot_general(
        hidden, rotated, (((0,), (0,)), ((), ())), preferred_element_type=jnp.float32
    )
    scaled = product.reshape(dp_size * shard_rows, block_count, BLOCK) * scales[:, :, None]
    summed = lax.psum_scatter(
        jnp.clip(scaled, -CLIP_LEVEL, CLIP_LEVEL)
        .reshape(dp_size * shard_rows, model_width)
        .astype(jnp.bfloat16),
        "dp",
        scatter_dimension=0,
        tiled=True,
    ).astype(jnp.float32)
    shard_scales = lax.dynamic_slice_in_dim(
        scales, lax.axis_index("dp") * shard_rows, shard_rows, 0
    )
    unscaled = summed.reshape(shard_rows, block_count, BLOCK) / shard_scales[:, :, None]
    decoded = jnp.einsum("rbj,jk->rbk", unscaled, matrix, precision=lax.Precision.HIGHEST)
    gradient = (decoded * sign_flips).reshape(shard_rows, model_width)
    new_one = BETA_ONE * moment_one + (1.0 - BETA_ONE) * gradient
    new_two = BETA_TWO * moment_two + (1.0 - BETA_TWO) * gradient * gradient
    update = new_one / FIRST_BIAS / (jnp.sqrt(new_two / SECOND_BIAS) + EPSILON)
    new_master = master - LEARN_RATE * (update + WEIGHT_DECAY * master)
    partial_value = jnp.dot(
        next_hidden,
        lax.all_gather(new_master.astype(jnp.bfloat16), "dp", axis=0, tiled=True),
        preferred_element_type=jnp.float32,
    )
    next_out = lax.psum_scatter(
        partial_value.astype(jnp.bfloat16), "tensor", scatter_dimension=0, tiled=True
    )
    return (gradient, new_master, new_one, new_two, next_out)


def solution(mesh):
    grouped = mesh.shape["dp"] == 8 and mesh.shape["tensor"] == 4
    return jax.shard_map(
        on_device if grouped else general,
        mesh=mesh,
        in_specs=(
            P("dp", "tensor"),
            P("dp", "tensor"),
            P("dp", None),
            P(),
            P("tensor", None),
            P(("tensor", "dp"), None),
            P(("tensor", "dp"), None),
            P(("tensor", "dp"), None),
        ),
        out_specs=(
            P(("tensor", "dp"), None),
            P(("tensor", "dp"), None),
            P(("tensor", "dp"), None),
            P(("tensor", "dp"), None),
            P(("dp", "tensor"), None),
        ),
        check_vma=False,
    )
```

```python
import math

import jax
import jax.numpy as jnp
import numpy as np
from jax import lax
from jax.experimental import pallas as pl
from jax.experimental.pallas import tpu as pltpu
from jax.sharding import PartitionSpec as P

BLOCK = 256


CLIP_LEVEL = 127.0
LEARN_RATE = 0.005
BETA_ONE = 0.9
BETA_TWO = 0.95
WEIGHT_DECAY = 0.1
EPSILON = 1e-08
FIRST_BIAS = 1.0 - (0.9**50) ** 2
SECOND_BIAS = 1.0 - (0.95**50) ** 2
LEVELS = (16.0, 32.0, 64.0, 128.0)
CHUNKS = 4
GROUPS = 4
ADAM_STEPS = 2
FORWARD_STEPS = 2
ORDER = (
    "rot",
    "tu0",
    "g10",
    "tu3",
    "g11",
    "tu2",
    "g12",
    "ay0",
    "g13",
    "ay1",
    "ad0",
    "tu1",
    "ay2",
    "ad1",
    "g20",
    "ay3",
    "ad2",
    "g21",
    "sc0",
    "ad3",
    "g22",
    "sc1",
    "sx0",
    "g23",
    "sc2",
    "sx1",
    "sn0",
    "sc3",
    "sx2",
    "sn1",
    "sx3",
    "sn2",
    "sn3",
)
COST = {"ro": 300000000, "st": 25000000000, "ay": 300000000, "g1": 300000000, "ad": 300000000, "tu": 300000000, "g2": 300000000, "sc": 300000000, "sx": 300000000, "sn": 300000000}
VMEM_BYTES = 28 * 1024 * 1024


def hadamard(block_size):
    positions = np.arange(block_size)
    common_bits = positions[:, None] & positions[None, :]
    parity = np.zeros((block_size, block_size), np.int32)
    for bit_shift in range(block_size.bit_length() - 1):
        parity += (common_bits >> bit_shift) & 1
    return ((1 - 2 * (parity & 1)) / math.sqrt(block_size)).astype(np.float32)


def dot(a, b):
    return lax.dot_general(a, b, (((1,), (0,)), ((), ())), preferred_element_type=jnp.float32)


def block_spec(shape, index_map):
    return pl.BlockSpec(shape, index_map)


def whole(shape):
    return pl.BlockSpec(shape, lambda i, p: (0,) * len(shape))


class Chain:
    def __init__(self, place):
        self.place = place
        self.held = []

    def note(self, value):
        self.held.append(value)

    def __call__(self, name, body, grid, in_specs, out_specs, out_shape, scratch, args, aliases=None, token=0):
        held = self.held
        count, extra = len(args), len(held)

        def wrapped(place_ref, *refs):
            body(place_ref, *refs[:count], *refs[count + extra :])

        outs = pl.pallas_call(
            wrapped,
            grid_spec=pltpu.PrefetchScalarGridSpec(
                num_scalar_prefetch=1,
                grid=grid,
                in_specs=list(in_specs) + [pl.BlockSpec(memory_space=pl.ANY)] * extra,
                out_specs=out_specs,
                scratch_shapes=scratch,
            ),
            out_shape=out_shape,
            input_output_aliases=aliases or {},
            compiler_params=pltpu.CompilerParams(vmem_limit_bytes=VMEM_BYTES),
            cost_estimate=pl.CostEstimate(flops=COST[name[:2]], bytes_accessed=1000, transcendentals=0),
        )(self.place, *args, *held)
        self.held = [outs[token]]
        return outs


def rotate(chain, out_grad, flips, matrix):
    rows, width = out_grad.shape
    step = width // CHUNKS
    piece = step // 4
    per_group = CHUNKS // GROUPS

    def body(place_ref, grad_ref, flips_ref, matrix_ref, out_ref, *own_refs):
        position = place_ref[0]
        for block in range(step // BLOCK):
            columns = slice(block * BLOCK, (block + 1) * BLOCK)
            signed = grad_ref[:, columns] * flips_ref[block]
            out_ref[:, columns] = dot(signed, matrix_ref[...]).astype(jnp.bfloat16)
        for chunk in range(CHUNKS):

            @pl.when(pl.program_id(0) == chunk)
            def _():
                start = (chunk % per_group) * piece
                own = out_ref[:, pl.ds(pl.multiple_of(position * piece, BLOCK), piece)]
                own_refs[chunk // per_group][:, start : start + piece] = own

    return chain(
        "rot",
        body,
        (CHUNKS,),
        [
            block_spec((rows, step), lambda b, p: (0, b)),
            block_spec((step // BLOCK, 1, BLOCK), lambda b, p: (b, 0, 0)),
            whole((BLOCK, BLOCK)),
        ],
        [block_spec((rows, step), lambda b, p: (0, b))] + [whole((rows, per_group * piece))] * GROUPS,
        [jax.ShapeDtypeStruct((rows, width), jnp.bfloat16)]
        + [jax.ShapeDtypeStruct((rows, per_group * piece), jnp.bfloat16)] * GROUPS,
        [],
        (out_grad, flips.reshape(width // BLOCK, 1, BLOCK), matrix),
    )


def coded_sum(chain, chunk, hidden_parts, rotated, pieces, scales):
    units, tokens = hidden_parts[0].shape
    rows = units // 2
    width = rotated.shape[1] // CHUNKS
    piece = width // 4
    block_count = scales.shape[1]

    def body(place_ref, h0, h1, g0, g1, own_ref, u_ref, cu_ref, v_ref, cv_ref, scales_ref, keep_ref, send_ref, acc_ref):
        position, y = place_ref[0], place_ref[1]
        mine = pl.ds(pl.multiple_of(y * rows, 8), rows)
        theirs = pl.ds(pl.multiple_of((1 - y) * rows, 8), rows)
        lane = lax.broadcasted_iota(jnp.int32, (2 * rows, block_count), 1)
        all_scales = scales_ref[...]
        for j, ref in enumerate((u_ref, cu_ref, v_ref, cv_ref)):
            quarter = jnp.bitwise_xor(position, j)
            for part in range(piece // BLOCK):
                column = pl.multiple_of(quarter * piece + part * BLOCK, BLOCK)
                columns = pl.ds(column, BLOCK)
                block = chunk * (width // BLOCK) + quarter * (piece // BLOCK) + part
                scale = jnp.sum(jnp.where(lane == block, all_scales, 0.0), axis=1, keepdims=True)

                def coded(hidden, values):
                    product = dot(hidden, values) * scale
                    return jnp.clip(product, -CLIP_LEVEL, CLIP_LEVEL).astype(jnp.bfloat16).astype(jnp.float32)

                values, other = own_ref[:, columns], ref[:, part * BLOCK : (part + 1) * BLOCK]

                @pl.when(pl.program_id(0) == 0)
                def _():
                    acc_ref[...] = coded(h0[...], values) + coded(g0[...], other)

                @pl.when(pl.program_id(0) == 1)
                def _():
                    acc_ref[...] = coded(h1[...], values) + coded(g1[...], other)

                keep_ref[0, :, columns] = acc_ref[mine, :].astype(jnp.bfloat16)
                send_ref[0, :, columns] = acc_ref[theirs, :].astype(jnp.bfloat16)

    out = jax.ShapeDtypeStruct((2, rows, width), jnp.bfloat16)
    part_spec = block_spec((tokens, piece), lambda i, p: (0, chunk % (CHUNKS // GROUPS)))
    return chain(
        f"g1{chunk}",
        body,
        (2,),
        [whole((units, tokens))] * 4
        + [block_spec((tokens, width), lambda i, p: (0, chunk))]
        + [part_spec] * 4
        + [block_spec((2 * rows, block_count), lambda i, p: (i, 0))],
        [block_spec((1, rows, width), lambda i, p: (jnp.bitwise_xor(i, p[2]), 0, 0))] * 2,
        [out, out],
        [pltpu.VMEM((2 * rows, BLOCK), jnp.float32)],
        (*hidden_parts, rotated, *pieces, scales),
    )


def adam(chain, chunk, kept, received, shard_scales, flips, matrix, master, one, two, previous):
    rows, width = kept.shape
    model_width = master.shape[1]
    block_count = shard_scales.shape[1]
    step = width // ADAM_STEPS
    parts = step // BLOCK
    chained = previous is not None

    def body(place_ref, kept_ref, received_ref, scales_ref, flips_ref, matrix_ref, master_ref, one_ref, two_ref, *rest):
        grad_out, master_out, one_out, two_out, weight_out = rest[-5:]
        lane = lax.broadcasted_iota(jnp.int32, (rows, block_count), 1)
        all_scales = scales_ref[...]
        for part in range(parts):
            block = (chunk * ADAM_STEPS + pl.program_id(0)) * parts + part
            columns = slice(part * BLOCK, (part + 1) * BLOCK)
            scale = jnp.sum(jnp.where(lane == block, all_scales, 0.0), axis=1, keepdims=True)
            decoded = dot(kept_ref[:, columns], matrix_ref[...]) + dot(received_ref[:, columns], matrix_ref[...])
            gradient = decoded / scale * flips_ref[part]
            new_one = BETA_ONE * one_ref[:, columns] + (1.0 - BETA_ONE) * gradient
            new_two = BETA_TWO * two_ref[:, columns] + (1.0 - BETA_TWO) * gradient * gradient
            update = new_one / FIRST_BIAS / (jnp.sqrt(new_two / SECOND_BIAS) + EPSILON)
            old = master_ref[:, columns]
            new_master = old - LEARN_RATE * (update + WEIGHT_DECAY * old)
            grad_out[:, columns] = gradient
            master_out[:, columns] = new_master
            one_out[:, columns] = new_one
            two_out[:, columns] = new_two
            weight_out[:, columns] = new_master.astype(jnp.bfloat16)

    local = block_spec((rows, step), lambda j, p: (0, j))
    placed = block_spec((rows, step), lambda j, p: (0, chunk * ADAM_STEPS + j))
    state = jax.ShapeDtypeStruct((rows, model_width), jnp.float32)
    return chain(
        f"ad{chunk}",
        body,
        (ADAM_STEPS,),
        [
            local,
            local,
            whole((rows, block_count)),
            block_spec((parts, 1, BLOCK), lambda j, p: (chunk * ADAM_STEPS + j, 0, 0)),
            whole((BLOCK, BLOCK)),
            placed,
            placed,
            placed,
        ]
        + ([pl.BlockSpec(memory_space=pl.ANY)] * 4 if chained else []),
        [placed] * 4 + [local],
        [state] * 4 + [jax.ShapeDtypeStruct((rows, width), jnp.bfloat16)],
        [],
        (
            kept,
            received,
            shard_scales,
            flips.astype(jnp.float32).reshape(block_count, 1, BLOCK),
            matrix,
            *(pltpu.with_memory_space_constraint(value, pltpu.HBM) for value in (master, one, two)),
            *(previous if chained else ()),
        ),
        {9 + i: i for i in range(4)} if chained else None,
        token=4,
    )


def forward(chain, name, inputs, weight, other):
    tokens, units = inputs[0].shape
    rows, width = weight.shape
    quarter = tokens // 4
    step = width // FORWARD_STEPS

    def body(place_ref, n0, n1, n2, n3, weight_ref, other_ref, o0, o1, o2, o3, acc_ref, joined_ref):
        position, y = place_ref[0], place_ref[1]
        joined_ref[pl.ds(pl.multiple_of(y * rows, 8), rows), :] = weight_ref[...].astype(jnp.float32)
        joined_ref[pl.ds(pl.multiple_of((1 - y) * rows, 8), rows), :] = other_ref[...].astype(jnp.float32)
        joined = joined_ref[...].astype(jnp.bfloat16)
        for k, ref in enumerate((n0, n2, n1, n3)):
            acc_ref[...] = dot(ref[...], joined).astype(jnp.bfloat16)
            for i, out_ref in enumerate((o0, o1, o2, o3)):
                start = jnp.bitwise_xor(position, i) * quarter
                out_ref[k] = acc_ref[pl.ds(pl.multiple_of(start, quarter), quarter), :]

    return chain(
        name,
        body,
        (FORWARD_STEPS,),
        [whole((tokens, units))] * 4 + [block_spec((rows, step), lambda j, p: (0, j))] * 2,
        [block_spec((4, quarter, step), lambda j, p: (0, 0, j))] * 4,
        [jax.ShapeDtypeStruct((4, quarter, width), jnp.bfloat16)] * 4,
        [pltpu.VMEM((tokens, step), jnp.bfloat16), pltpu.VMEM((units, step), jnp.float32)],
        (*inputs, weight, other),
    )


def add(a, b):
    return (a.astype(jnp.float32) + b.astype(jnp.float32)).astype(jnp.bfloat16)


def on_device(
    hidden, next_hidden, out_grad, sign_bits, scale_index, master, moment_one, moment_two
):
    dp_size = lax.axis_size("dp")
    tensor_size = lax.axis_size("tensor")
    tokens = hidden.shape[0]
    shard_rows = master.shape[0]
    block_count = sign_bits.shape[0]
    replica = lax.axis_index("dp")
    group = lax.axis_index("tensor")
    z, y = replica // 2, replica % 2
    far_side = replica // 4
    place = jnp.stack([group, y, far_side]).astype(jnp.int32)
    matrix = jnp.asarray(hadamard(BLOCK)).astype(jnp.bfloat16)
    flips = (1 - 2 * sign_bits).astype(jnp.bfloat16)

    def over_dp(value, bits):
        return lax.ppermute(value, "dp", [(i, i ^ bits) for i in range(dp_size)])

    def over_tensor(value, bits):
        return lax.ppermute(value, "tensor", [(i, i ^ bits) for i in range(tensor_size)])

    units = 2 * shard_rows
    near_z = z % 2
    by_pair = hidden.T.reshape(2, 2, units, tokens)

    def pair_rows(values, k):
        picked = lax.dynamic_index_in_dim(values, near_z ^ k, 1, keepdims=False)
        return picked.reshape(2 * units, picked.shape[-1])

    hidden_parts = [lax.dynamic_index_in_dim(half, near_z, 0, keepdims=False) for half in by_pair]
    hidden_parts += [
        over_dp(lax.dynamic_index_in_dim(half, 1 - near_z, 0, keepdims=False), 2) for half in by_pair
    ]
    chain = Chain(place)
    rotated, *own_pieces = rotate(chain, out_grad, flips, matrix)

    level_table = jnp.array(LEVELS, jnp.float32)
    matches = (scale_index[:, :, None] == jnp.arange(4, dtype=jnp.int32)).astype(jnp.float32)
    all_scales = jnp.sum(matches * level_table, axis=-1) * math.sqrt(dp_size)
    scales = pair_rows(all_scales.reshape(2, 2, units, block_count), 0)
    shard_scales = lax.dynamic_slice_in_dim(scales, (2 * far_side + y) * shard_rows, shard_rows, 0)

    next_t = next_hidden.T
    inputs = [lax.dynamic_slice_in_dim(next_t, (z ^ k) * units, units, 0) for k in range(4)]
    inputs = [inputs[0]] + [over_dp(inputs[k], 2 * k) for k in range(1, 4)]

    state = None
    pieces, kept, halves, arriving, weights, partials, sums, nears, outs = ({} for _ in range(9))
    turned_inputs = {}

    def gather(k):
        u = over_dp(own_pieces[k], 2)
        v = over_tensor(u, 2)
        pieces[k] = (u, over_tensor(u, 1), v, over_tensor(v, 1))

    def first(k):
        kept[k], sent = coded_sum(chain, k, hidden_parts, rotated, pieces[k // (CHUNKS // GROUPS)], scales)
        halves[k] = over_dp(sent, 1)

    def join_rows(k):
        go = add(kept[k][1], halves[k][1])
        kept[k] = add(kept[k][0], halves[k][0])
        arriving[k] = over_dp(go, 4)
        chain.note(go)

    def update(k):
        nonlocal state
        *state, weight = adam(
            chain, k, kept[k], arriving[k], shard_scales, flips, matrix, master, moment_one, moment_two, state
        )
        weights[k] = (weight, over_dp(weight, 1))

    def turn(k):
        turned_inputs[k] = inputs[k].T
        chain.note(inputs[k])

    def second(k):
        stay, near, go, far = forward(chain, f"g2{k}", [turned_inputs[i] for i in range(4)], *weights[k])
        partials[k] = (stay, go, over_tensor(near, 1), over_tensor(far, 1))

    def sum_cores(k):
        stay, go, near, far = partials[k]
        go = add(go, far)
        sums[k] = (add(stay, near), over_tensor(go, 2))
        chain.note(go)

    def sum_chips(k):
        stay, more = sums[k]
        go = add(stay[2:], more[2:])
        nears[k] = (add(stay[:2], more[:2]), over_dp(go, 2))
        chain.note(go)

    def sum_near(k):
        stay, more = nears[k]
        go = add(stay[1], more[1])
        outs[k] = (add(stay[0], more[0]), over_dp(go, 4))
        chain.note(go)

    steps = {"tu": turn, "ay": join_rows, "g1": first, "ad": update, "g2": second, "sc": sum_cores, "sx": sum_chips, "sn": sum_near}
    for group_index in range(GROUPS):
        gather(group_index)
    for name in ORDER[1:]:
        steps[name[:2]](int(name[2:]))
    next_out = jnp.concatenate([add(*outs[k]) for k in range(CHUNKS)], axis=1)
    gradient, new_master, new_one, new_two = state
    return (gradient, new_master, new_one, new_two, next_out)


def general(
    hidden, next_hidden, out_grad, sign_bits, scale_index, master, moment_one, moment_two
):
    dp_size = lax.axis_size("dp")
    tok_rows = hidden.shape[0]
    model_width = out_grad.shape[1]
    block_count = sign_bits.shape[0]
    shard_rows = master.shape[0]
    matrix = jnp.asarray(hadamard(BLOCK))
    sign_flips = (1 - 2 * sign_bits).astype(jnp.float32)
    signed = out_grad.reshape(tok_rows, block_count, BLOCK) * sign_flips.astype(jnp.bfloat16)
    rotated = jnp.einsum(
        "tbj,jk->tbk", signed, matrix.astype(jnp.bfloat16), preferred_element_type=jnp.float32
    )
    rotated = rotated.astype(jnp.bfloat16).reshape(tok_rows, model_width)
    level_table = jnp.array(LEVELS, jnp.float32)
    matches = (scale_index[:, :, None] == jnp.arange(4, dtype=jnp.int32)).astype(jnp.float32)
    scales = jnp.sum(matches * level_table, axis=-1) * math.sqrt(dp_size)
    product = lax.dot_general(
        hidden, rotated, (((0,), (0,)), ((), ())), preferred_element_type=jnp.float32
    )
    scaled = product.reshape(dp_size * shard_rows, block_count, BLOCK) * scales[:, :, None]
    summed = lax.psum_scatter(
        jnp.clip(scaled, -CLIP_LEVEL, CLIP_LEVEL)
        .reshape(dp_size * shard_rows, model_width)
        .astype(jnp.bfloat16),
        "dp",
        scatter_dimension=0,
        tiled=True,
    ).astype(jnp.float32)
    shard_scales = lax.dynamic_slice_in_dim(
        scales, lax.axis_index("dp") * shard_rows, shard_rows, 0
    )
    unscaled = summed.reshape(shard_rows, block_count, BLOCK) / shard_scales[:, :, None]
    decoded = jnp.einsum("rbj,jk->rbk", unscaled, matrix, precision=lax.Precision.HIGHEST)
    gradient = (decoded * sign_flips).reshape(shard_rows, model_width)
    new_one = BETA_ONE * moment_one + (1.0 - BETA_ONE) * gradient
    new_two = BETA_TWO * moment_two + (1.0 - BETA_TWO) * gradient * gradient
    update = new_one / FIRST_BIAS / (jnp.sqrt(new_two / SECOND_BIAS) + EPSILON)
    new_master = master - LEARN_RATE * (update + WEIGHT_DECAY * master)
    partial_value = jnp.dot(
        next_hidden,
        lax.all_gather(new_master.astype(jnp.bfloat16), "dp", axis=0, tiled=True),
        preferred_element_type=jnp.float32,
    )
    next_out = lax.psum_scatter(
        partial_value.astype(jnp.bfloat16), "tensor", scatter_dimension=0, tiled=True
    )
    return (gradient, new_master, new_one, new_two, next_out)


def solution(mesh):
    grouped = mesh.shape["dp"] == 8 and mesh.shape["tensor"] == 4
    return jax.shard_map(
        on_device if grouped else general,
        mesh=mesh,
        in_specs=(
            P("dp", "tensor"),
            P("dp", "tensor"),
            P("dp", None),
            P(),
            P("tensor", None),
            P(("tensor", "dp"), None),
            P(("tensor", "dp"), None),
            P(("tensor", "dp"), None),
        ),
        out_specs=(
            P(("tensor", "dp"), None),
            P(("tensor", "dp"), None),
            P(("tensor", "dp"), None),
            P(("tensor", "dp"), None),
            P(("dp", "tensor"), None),
        ),
        check_vma=False,
    )
```

```python
import math

import jax
import jax.numpy as jnp
import numpy as np
from jax import lax
from jax.experimental import pallas as pl
from jax.experimental.pallas import tpu as pltpu
from jax.sharding import PartitionSpec as P

BLOCK = 256


CLIP_LEVEL = 127.0
LEARN_RATE = 0.005
BETA_ONE = 0.9
BETA_TWO = 0.95
WEIGHT_DECAY = 0.1
EPSILON = 1e-08
FIRST_BIAS = 1.0 - (0.9**50) ** 2
SECOND_BIAS = 1.0 - (0.95**50) ** 2
LEVELS = (16.0, 32.0, 64.0, 128.0)
CHUNKS = 4
GROUPS = 4
ADAM_STEPS = 2
FORWARD_STEPS = 2
ORDER = (
    "rot",
    "tu0",
    "g10",
    "tu3",
    "g11",
    "tu2",
    "g12",
    "ay0",
    "g13",
    "ay1",
    "ad0",
    "tu1",
    "ay2",
    "ad1",
    "g20",
    "ay3",
    "ad2",
    "g21",
    "sc0",
    "ad3",
    "g22",
    "sc1",
    "sx0",
    "g23",
    "sc2",
    "sx1",
    "sn0",
    "sc3",
    "sx2",
    "sn1",
    "sx3",
    "sn2",
    "sn3",
)
COST = {"ro": 300000000, "st": 25000000000, "ay": 300000000, "g1": 300000000, "ad": 300000000, "tu": 300000000, "g2": 300000000, "sc": 300000000, "sx": 300000000, "sn": 300000000}
VMEM_BYTES = 28 * 1024 * 1024


def hadamard(block_size):
    positions = np.arange(block_size)
    common_bits = positions[:, None] & positions[None, :]
    parity = np.zeros((block_size, block_size), np.int32)
    for bit_shift in range(block_size.bit_length() - 1):
        parity += (common_bits >> bit_shift) & 1
    return ((1 - 2 * (parity & 1)) / math.sqrt(block_size)).astype(np.float32)


def dot(a, b):
    return lax.dot_general(a, b, (((1,), (0,)), ((), ())), preferred_element_type=jnp.float32)


def block_spec(shape, index_map):
    return pl.BlockSpec(shape, index_map)


def whole(shape):
    return pl.BlockSpec(shape, lambda i, p: (0,) * len(shape))


class Chain:
    def __init__(self, place):
        self.place = place
        self.held = []

    def note(self, value):
        self.held.append(value)

    def __call__(self, name, body, grid, in_specs, out_specs, out_shape, scratch, args, aliases=None, token=0):
        held = self.held
        count, extra = len(args), len(held)

        def wrapped(place_ref, *refs):
            body(place_ref, *refs[:count], *refs[count + extra :])

        outs = pl.pallas_call(
            wrapped,
            grid_spec=pltpu.PrefetchScalarGridSpec(
                num_scalar_prefetch=1,
                grid=grid,
                in_specs=list(in_specs) + [pl.BlockSpec(memory_space=pl.ANY)] * extra,
                out_specs=out_specs,
                scratch_shapes=scratch,
            ),
            out_shape=out_shape,
            input_output_aliases=aliases or {},
            compiler_params=pltpu.CompilerParams(vmem_limit_bytes=VMEM_BYTES),
            cost_estimate=pl.CostEstimate(flops=COST[name[:2]], bytes_accessed=1000, transcendentals=0),
        )(self.place, *args, *held)
        self.held = [outs[token]]
        return outs


def rotate(chain, out_grad, flips, matrix):
    rows, width = out_grad.shape
    step = width // CHUNKS
    piece = step // 4
    per_group = CHUNKS // GROUPS

    def body(place_ref, grad_ref, flips_ref, matrix_ref, out_ref, *own_refs):
        position = place_ref[0]
        for block in range(step // BLOCK):
            columns = slice(block * BLOCK, (block + 1) * BLOCK)
            signed = grad_ref[:, columns] * flips_ref[block]
            out_ref[:, columns] = dot(signed, matrix_ref[...]).astype(jnp.bfloat16)
        for chunk in range(CHUNKS):

            @pl.when(pl.program_id(0) == chunk)
            def _():
                start = (chunk % per_group) * piece
                own = out_ref[:, pl.ds(pl.multiple_of(position * piece, BLOCK), piece)]
                own_refs[chunk // per_group][:, start : start + piece] = own

    return chain(
        "rot",
        body,
        (CHUNKS,),
        [
            block_spec((rows, step), lambda b, p: (0, b)),
            block_spec((step // BLOCK, 1, BLOCK), lambda b, p: (b, 0, 0)),
            whole((BLOCK, BLOCK)),
        ],
        [block_spec((rows, step), lambda b, p: (0, b))] + [whole((rows, per_group * piece))] * GROUPS,
        [jax.ShapeDtypeStruct((rows, width), jnp.bfloat16)]
        + [jax.ShapeDtypeStruct((rows, per_group * piece), jnp.bfloat16)] * GROUPS,
        [],
        (out_grad, flips.reshape(width // BLOCK, 1, BLOCK), matrix),
    )


def coded_sum(chain, chunk, hidden_parts, rotated, pieces, scales):
    units, tokens = hidden_parts[1].shape
    rows = units // 2
    width = rotated.shape[1] // CHUNKS
    piece = width // 4
    block_count = scales.shape[1]

    def body(place_ref, own_hidden, near_hidden, far_hidden, own_ref, u_ref, cu_ref, v_ref, cv_ref, scales_ref, keep_ref, send_ref, acc_ref):
        position, y = place_ref[0], place_ref[1]
        mine = pl.ds(pl.multiple_of(y * rows, 8), rows)
        theirs = pl.ds(pl.multiple_of((1 - y) * rows, 8), rows)
        lane = lax.broadcasted_iota(jnp.int32, (2 * rows, block_count), 1)
        all_scales = scales_ref[...]
        received = jnp.where(pl.program_id(0) == 0, near_hidden[...], far_hidden[...])
        for j, ref in enumerate((u_ref, cu_ref, v_ref, cv_ref)):
            quarter = jnp.bitwise_xor(position, j)
            for part in range(piece // BLOCK):
                column = pl.multiple_of(quarter * piece + part * BLOCK, BLOCK)
                columns = pl.ds(column, BLOCK)
                block = chunk * (width // BLOCK) + quarter * (piece // BLOCK) + part
                scale = jnp.sum(jnp.where(lane == block, all_scales, 0.0), axis=1, keepdims=True)

                def coded(hidden, values):
                    product = dot(hidden, values) * scale
                    return jnp.clip(product, -CLIP_LEVEL, CLIP_LEVEL).astype(jnp.bfloat16).astype(jnp.float32)

                values, other = own_ref[:, columns], ref[:, part * BLOCK : (part + 1) * BLOCK]

                acc_ref[...] = coded(own_hidden[...], values) + coded(received, other)
                keep_ref[0, :, columns] = acc_ref[mine, :].astype(jnp.bfloat16)
                send_ref[0, :, columns] = acc_ref[theirs, :].astype(jnp.bfloat16)

    out = jax.ShapeDtypeStruct((2, rows, width), jnp.bfloat16)
    part_spec = block_spec((tokens, piece), lambda i, p: (0, chunk % (CHUNKS // GROUPS)))
    return chain(
        f"g1{chunk}",
        body,
        (2,),
        [block_spec((units, tokens), lambda i, p: (i, 0))]
        + [whole((units, tokens))] * 2
        + [block_spec((tokens, width), lambda i, p: (0, chunk))]
        + [part_spec] * 4
        + [block_spec((2 * rows, block_count), lambda i, p: (i, 0))],
        [block_spec((1, rows, width), lambda i, p: (jnp.bitwise_xor(i, p[2]), 0, 0))] * 2,
        [out, out],
        [pltpu.VMEM((2 * rows, BLOCK), jnp.float32)],
        (*hidden_parts, rotated, *pieces, scales),
    )


def adam(chain, chunk, kept, received, shard_scales, flips, matrix, master, one, two, previous):
    rows, width = kept.shape
    model_width = master.shape[1]
    block_count = shard_scales.shape[1]
    step = width // ADAM_STEPS
    parts = step // BLOCK
    chained = previous is not None

    def body(place_ref, kept_ref, received_ref, scales_ref, flips_ref, matrix_ref, master_ref, one_ref, two_ref, *rest):
        grad_out, master_out, one_out, two_out, weight_out = rest[-5:]
        lane = lax.broadcasted_iota(jnp.int32, (rows, block_count), 1)
        all_scales = scales_ref[...]
        for part in range(parts):
            block = (chunk * ADAM_STEPS + pl.program_id(0)) * parts + part
            columns = slice(part * BLOCK, (part + 1) * BLOCK)
            scale = jnp.sum(jnp.where(lane == block, all_scales, 0.0), axis=1, keepdims=True)
            decoded = dot(kept_ref[:, columns], matrix_ref[...]) + dot(received_ref[:, columns], matrix_ref[...])
            gradient = decoded / scale * flips_ref[part]
            new_one = BETA_ONE * one_ref[:, columns] + (1.0 - BETA_ONE) * gradient
            new_two = BETA_TWO * two_ref[:, columns] + (1.0 - BETA_TWO) * gradient * gradient
            update = new_one / FIRST_BIAS / (jnp.sqrt(new_two / SECOND_BIAS) + EPSILON)
            old = master_ref[:, columns]
            new_master = old - LEARN_RATE * (update + WEIGHT_DECAY * old)
            grad_out[:, columns] = gradient
            master_out[:, columns] = new_master
            one_out[:, columns] = new_one
            two_out[:, columns] = new_two
            weight_out[:, columns] = new_master.astype(jnp.bfloat16)

    local = block_spec((rows, step), lambda j, p: (0, j))
    placed = block_spec((rows, step), lambda j, p: (0, chunk * ADAM_STEPS + j))
    state = jax.ShapeDtypeStruct((rows, model_width), jnp.float32)
    return chain(
        f"ad{chunk}",
        body,
        (ADAM_STEPS,),
        [
            local,
            local,
            whole((rows, block_count)),
            block_spec((parts, 1, BLOCK), lambda j, p: (chunk * ADAM_STEPS + j, 0, 0)),
            whole((BLOCK, BLOCK)),
            placed,
            placed,
            placed,
        ]
        + ([pl.BlockSpec(memory_space=pl.ANY)] * 4 if chained else []),
        [placed] * 4 + [local],
        [state] * 4 + [jax.ShapeDtypeStruct((rows, width), jnp.bfloat16)],
        [],
        (
            kept,
            received,
            shard_scales,
            flips.astype(jnp.float32).reshape(block_count, 1, BLOCK),
            matrix,
            *(pltpu.with_memory_space_constraint(value, pltpu.HBM) for value in (master, one, two)),
            *(previous if chained else ()),
        ),
        {9 + i: i for i in range(4)} if chained else None,
        token=4,
    )


def forward(chain, name, inputs, weight, other):
    tokens, units = inputs[0].shape
    rows, width = weight.shape
    quarter = tokens // 4
    step = width // FORWARD_STEPS

    def body(place_ref, n0, n1, n2, n3, weight_ref, other_ref, o0, o1, o2, o3, acc_ref, joined_ref):
        position, y = place_ref[0], place_ref[1]
        joined_ref[pl.ds(pl.multiple_of(y * rows, 8), rows), :] = weight_ref[...].astype(jnp.float32)
        joined_ref[pl.ds(pl.multiple_of((1 - y) * rows, 8), rows), :] = other_ref[...].astype(jnp.float32)
        joined = joined_ref[...].astype(jnp.bfloat16)
        for k, ref in enumerate((n0, n2, n1, n3)):
            acc_ref[...] = dot(ref[...], joined).astype(jnp.bfloat16)
            for i, out_ref in enumerate((o0, o1, o2, o3)):
                start = jnp.bitwise_xor(position, i) * quarter
                out_ref[k] = acc_ref[pl.ds(pl.multiple_of(start, quarter), quarter), :]

    return chain(
        name,
        body,
        (FORWARD_STEPS,),
        [whole((tokens, units))] * 4 + [block_spec((rows, step), lambda j, p: (0, j))] * 2,
        [block_spec((4, quarter, step), lambda j, p: (0, 0, j))] * 4,
        [jax.ShapeDtypeStruct((4, quarter, width), jnp.bfloat16)] * 4,
        [pltpu.VMEM((tokens, step), jnp.bfloat16), pltpu.VMEM((units, step), jnp.float32)],
        (*inputs, weight, other),
    )


def add(a, b):
    return (a.astype(jnp.float32) + b.astype(jnp.float32)).astype(jnp.bfloat16)


def on_device(
    hidden, next_hidden, out_grad, sign_bits, scale_index, master, moment_one, moment_two
):
    dp_size = lax.axis_size("dp")
    tensor_size = lax.axis_size("tensor")
    tokens = hidden.shape[0]
    shard_rows = master.shape[0]
    block_count = sign_bits.shape[0]
    replica = lax.axis_index("dp")
    group = lax.axis_index("tensor")
    z, y = replica // 2, replica % 2
    far_side = replica // 4
    place = jnp.stack([group, y, far_side]).astype(jnp.int32)
    matrix = jnp.asarray(hadamard(BLOCK)).astype(jnp.bfloat16)
    flips = (1 - 2 * sign_bits).astype(jnp.bfloat16)

    def over_dp(value, bits):
        return lax.ppermute(value, "dp", [(i, i ^ bits) for i in range(dp_size)])

    def over_tensor(value, bits):
        return lax.ppermute(value, "tensor", [(i, i ^ bits) for i in range(tensor_size)])

    units = 2 * shard_rows
    near_z = z % 2
    by_pair = hidden.T.reshape(2, 2, units, tokens)

    def pair_rows(values, k):
        picked = lax.dynamic_index_in_dim(values, near_z ^ k, 1, keepdims=False)
        return picked.reshape(2 * units, picked.shape[-1])

    hidden_parts = [pair_rows(by_pair, 0)] + [
        over_dp(lax.dynamic_index_in_dim(half, 1 - near_z, 0, keepdims=False), 2) for half in by_pair
    ]
    chain = Chain(place)
    rotated, *own_pieces = rotate(chain, out_grad, flips, matrix)

    level_table = jnp.array(LEVELS, jnp.float32)
    matches = (scale_index[:, :, None] == jnp.arange(4, dtype=jnp.int32)).astype(jnp.float32)
    all_scales = jnp.sum(matches * level_table, axis=-1) * math.sqrt(dp_size)
    scales = pair_rows(all_scales.reshape(2, 2, units, block_count), 0)
    shard_scales = lax.dynamic_slice_in_dim(scales, (2 * far_side + y) * shard_rows, shard_rows, 0)

    next_t = next_hidden.T
    inputs = [lax.dynamic_slice_in_dim(next_t, (z ^ k) * units, units, 0) for k in range(4)]
    inputs = [inputs[0]] + [over_dp(inputs[k], 2 * k) for k in range(1, 4)]

    state = None
    pieces, kept, halves, arriving, weights, partials, sums, nears, outs = ({} for _ in range(9))
    turned_inputs = {}

    def gather(k):
        u = over_dp(own_pieces[k], 2)
        v = over_tensor(u, 2)
        pieces[k] = (u, over_tensor(u, 1), v, over_tensor(v, 1))

    def first(k):
        kept[k], sent = coded_sum(chain, k, hidden_parts, rotated, pieces[k // (CHUNKS // GROUPS)], scales)
        halves[k] = over_dp(sent, 1)

    def join_rows(k):
        go = add(kept[k][1], halves[k][1])
        kept[k] = add(kept[k][0], halves[k][0])
        arriving[k] = over_dp(go, 4)
        chain.note(go)

    def update(k):
        nonlocal state
        *state, weight = adam(
            chain, k, kept[k], arriving[k], shard_scales, flips, matrix, master, moment_one, moment_two, state
        )
        weights[k] = (weight, over_dp(weight, 1))

    def turn(k):
        turned_inputs[k] = inputs[k].T
        chain.note(inputs[k])

    def second(k):
        stay, near, go, far = forward(chain, f"g2{k}", [turned_inputs[i] for i in range(4)], *weights[k])
        partials[k] = (stay, go, over_tensor(near, 1), over_tensor(far, 1))

    def sum_cores(k):
        stay, go, near, far = partials[k]
        go = add(go, far)
        sums[k] = (add(stay, near), over_tensor(go, 2))
        chain.note(go)

    def sum_chips(k):
        stay, more = sums[k]
        go = add(stay[2:], more[2:])
        nears[k] = (add(stay[:2], more[:2]), over_dp(go, 2))
        chain.note(go)

    def sum_near(k):
        stay, more = nears[k]
        go = add(stay[1], more[1])
        outs[k] = (add(stay[0], more[0]), over_dp(go, 4))
        chain.note(go)

    steps = {"tu": turn, "ay": join_rows, "g1": first, "ad": update, "g2": second, "sc": sum_cores, "sx": sum_chips, "sn": sum_near}
    for group_index in range(GROUPS):
        gather(group_index)
    for name in ORDER[1:]:
        steps[name[:2]](int(name[2:]))
    next_out = jnp.concatenate([add(*outs[k]) for k in range(CHUNKS)], axis=1)
    gradient, new_master, new_one, new_two = state
    return (gradient, new_master, new_one, new_two, next_out)


def general(
    hidden, next_hidden, out_grad, sign_bits, scale_index, master, moment_one, moment_two
):
    dp_size = lax.axis_size("dp")
    tok_rows = hidden.shape[0]
    model_width = out_grad.shape[1]
    block_count = sign_bits.shape[0]
    shard_rows = master.shape[0]
    matrix = jnp.asarray(hadamard(BLOCK))
    sign_flips = (1 - 2 * sign_bits).astype(jnp.float32)
    signed = out_grad.reshape(tok_rows, block_count, BLOCK) * sign_flips.astype(jnp.bfloat16)
    rotated = jnp.einsum(
        "tbj,jk->tbk", signed, matrix.astype(jnp.bfloat16), preferred_element_type=jnp.float32
    )
    rotated = rotated.astype(jnp.bfloat16).reshape(tok_rows, model_width)
    level_table = jnp.array(LEVELS, jnp.float32)
    matches = (scale_index[:, :, None] == jnp.arange(4, dtype=jnp.int32)).astype(jnp.float32)
    scales = jnp.sum(matches * level_table, axis=-1) * math.sqrt(dp_size)
    product = lax.dot_general(
        hidden, rotated, (((0,), (0,)), ((), ())), preferred_element_type=jnp.float32
    )
    scaled = product.reshape(dp_size * shard_rows, block_count, BLOCK) * scales[:, :, None]
    summed = lax.psum_scatter(
        jnp.clip(scaled, -CLIP_LEVEL, CLIP_LEVEL)
        .reshape(dp_size * shard_rows, model_width)
        .astype(jnp.bfloat16),
        "dp",
        scatter_dimension=0,
        tiled=True,
    ).astype(jnp.float32)
    shard_scales = lax.dynamic_slice_in_dim(
        scales, lax.axis_index("dp") * shard_rows, shard_rows, 0
    )
    unscaled = summed.reshape(shard_rows, block_count, BLOCK) / shard_scales[:, :, None]
    decoded = jnp.einsum("rbj,jk->rbk", unscaled, matrix, precision=lax.Precision.HIGHEST)
    gradient = (decoded * sign_flips).reshape(shard_rows, model_width)
    new_one = BETA_ONE * moment_one + (1.0 - BETA_ONE) * gradient
    new_two = BETA_TWO * moment_two + (1.0 - BETA_TWO) * gradient * gradient
    update = new_one / FIRST_BIAS / (jnp.sqrt(new_two / SECOND_BIAS) + EPSILON)
    new_master = master - LEARN_RATE * (update + WEIGHT_DECAY * master)
    partial_value = jnp.dot(
        next_hidden,
        lax.all_gather(new_master.astype(jnp.bfloat16), "dp", axis=0, tiled=True),
        preferred_element_type=jnp.float32,
    )
    next_out = lax.psum_scatter(
        partial_value.astype(jnp.bfloat16), "tensor", scatter_dimension=0, tiled=True
    )
    return (gradient, new_master, new_one, new_two, next_out)


def solution(mesh):
    grouped = mesh.shape["dp"] == 8 and mesh.shape["tensor"] == 4
    return jax.shard_map(
        on_device if grouped else general,
        mesh=mesh,
        in_specs=(
            P("dp", "tensor"),
            P("dp", "tensor"),
            P("dp", None),
            P(),
            P("tensor", None),
            P(("tensor", "dp"), None),
            P(("tensor", "dp"), None),
            P(("tensor", "dp"), None),
        ),
        out_specs=(
            P(("tensor", "dp"), None),
            P(("tensor", "dp"), None),
            P(("tensor", "dp"), None),
            P(("tensor", "dp"), None),
            P(("dp", "tensor"), None),
        ),
        check_vma=False,
    )
```

```python
import math

import jax
import jax.numpy as jnp
import numpy as np
from jax import lax
from jax.experimental import pallas as pl
from jax.experimental.pallas import tpu as pltpu
from jax.sharding import PartitionSpec as P

BLOCK = 256


CLIP_LEVEL = 127.0
LEARN_RATE = 0.005
BETA_ONE = 0.9
BETA_TWO = 0.95
WEIGHT_DECAY = 0.1
EPSILON = 1e-08
FIRST_BIAS = 1.0 - (0.9**50) ** 2
SECOND_BIAS = 1.0 - (0.95**50) ** 2
LEVELS = (16.0, 32.0, 64.0, 128.0)
CHUNKS = 4
GROUPS = 4
ADAM_STEPS = 2
FORWARD_STEPS = 2
ORDER = (
    "rot",
    "tu0",
    "g10",
    "tu3",
    "g11",
    "tu2",
    "g12",
    "ay0",
    "g13",
    "ay1",
    "ad0",
    "tu1",
    "ad1",
    "ay2",
    "g20",
    "ay3",
    "ad2",
    "g21",
    "sc0",
    "ad3",
    "g22",
    "sc1",
    "sx0",
    "g23",
    "sc2",
    "sx1",
    "sn0",
    "sc3",
    "sx2",
    "sn1",
    "sn2",
    "sx3",
    "sn3",
)
COST = {"ro": 300000000, "st": 25000000000, "ay": 300000000, "g1": 300000000, "ad": 300000000, "tu": 300000000, "g2": 300000000, "sc": 300000000, "sx": 300000000, "sn": 300000000, "ad1": 1000000, "g12": 3000000000}
VMEM_BYTES = 28 * 1024 * 1024


def hadamard(block_size):
    positions = np.arange(block_size)
    common_bits = positions[:, None] & positions[None, :]
    parity = np.zeros((block_size, block_size), np.int32)
    for bit_shift in range(block_size.bit_length() - 1):
        parity += (common_bits >> bit_shift) & 1
    return ((1 - 2 * (parity & 1)) / math.sqrt(block_size)).astype(np.float32)


def dot(a, b):
    return lax.dot_general(a, b, (((1,), (0,)), ((), ())), preferred_element_type=jnp.float32)


def block_spec(shape, index_map):
    return pl.BlockSpec(shape, index_map)


def whole(shape):
    return pl.BlockSpec(shape, lambda i, p: (0,) * len(shape))


class Chain:
    def __init__(self, place):
        self.place = place
        self.held = []

    def note(self, value):
        self.held.append(value)

    def __call__(self, name, body, grid, in_specs, out_specs, out_shape, scratch, args, aliases=None, token=0):
        held = self.held
        count, extra = len(args), len(held)

        def wrapped(place_ref, *refs):
            body(place_ref, *refs[:count], *refs[count + extra :])

        outs = pl.pallas_call(
            wrapped,
            grid_spec=pltpu.PrefetchScalarGridSpec(
                num_scalar_prefetch=1,
                grid=grid,
                in_specs=list(in_specs) + [pl.BlockSpec(memory_space=pl.ANY)] * extra,
                out_specs=out_specs,
                scratch_shapes=scratch,
            ),
            out_shape=out_shape,
            input_output_aliases=aliases or {},
            compiler_params=pltpu.CompilerParams(vmem_limit_bytes=VMEM_BYTES),
            cost_estimate=pl.CostEstimate(flops=COST.get(name, COST[name[:2]]), bytes_accessed=1000, transcendentals=0),
        )(self.place, *args, *held)
        self.held = [outs[token]]
        return outs


def rotate(chain, out_grad, flips, matrix):
    rows, width = out_grad.shape
    step = width // CHUNKS
    piece = step // 4
    per_group = CHUNKS // GROUPS

    def body(place_ref, grad_ref, flips_ref, matrix_ref, out_ref, *own_refs):
        position = place_ref[0]
        for block in range(step // BLOCK):
            columns = slice(block * BLOCK, (block + 1) * BLOCK)
            signed = grad_ref[:, columns] * flips_ref[block]
            out_ref[:, columns] = dot(signed, matrix_ref[...]).astype(jnp.bfloat16)
        for chunk in range(CHUNKS):

            @pl.when(pl.program_id(0) == chunk)
            def _():
                start = (chunk % per_group) * piece
                own = out_ref[:, pl.ds(pl.multiple_of(position * piece, BLOCK), piece)]
                own_refs[chunk // per_group][:, start : start + piece] = own

    return chain(
        "rot",
        body,
        (CHUNKS,),
        [
            block_spec((rows, step), lambda b, p: (0, b)),
            block_spec((step // BLOCK, 1, BLOCK), lambda b, p: (b, 0, 0)),
            whole((BLOCK, BLOCK)),
        ],
        [block_spec((rows, step), lambda b, p: (0, b))] + [whole((rows, per_group * piece))] * GROUPS,
        [jax.ShapeDtypeStruct((rows, width), jnp.bfloat16)]
        + [jax.ShapeDtypeStruct((rows, per_group * piece), jnp.bfloat16)] * GROUPS,
        [],
        (out_grad, flips.reshape(width // BLOCK, 1, BLOCK), matrix),
    )


def coded_sum(chain, chunk, hidden_parts, rotated, pieces, scales):
    units, tokens = hidden_parts[1].shape
    rows = units // 2
    width = rotated.shape[1] // CHUNKS
    piece = width // 4
    block_count = scales.shape[1]

    def body(place_ref, own_hidden, near_hidden, far_hidden, own_ref, u_ref, cu_ref, v_ref, cv_ref, scales_ref, keep_ref, send_ref, acc_ref):
        position, y = place_ref[0], place_ref[1]
        mine = pl.ds(pl.multiple_of(y * rows, 8), rows)
        theirs = pl.ds(pl.multiple_of((1 - y) * rows, 8), rows)
        lane = lax.broadcasted_iota(jnp.int32, (2 * rows, block_count), 1)
        all_scales = scales_ref[...]
        received = jnp.where(pl.program_id(0) == 0, near_hidden[...], far_hidden[...])
        for j, ref in enumerate((u_ref, cu_ref, v_ref, cv_ref)):
            quarter = jnp.bitwise_xor(position, j)
            for part in range(piece // BLOCK):
                column = pl.multiple_of(quarter * piece + part * BLOCK, BLOCK)
                columns = pl.ds(column, BLOCK)
                block = chunk * (width // BLOCK) + quarter * (piece // BLOCK) + part
                scale = jnp.sum(jnp.where(lane == block, all_scales, 0.0), axis=1, keepdims=True)

                def coded(hidden, values):
                    product = dot(hidden, values) * scale
                    return jnp.clip(product, -CLIP_LEVEL, CLIP_LEVEL).astype(jnp.bfloat16).astype(jnp.float32)

                values, other = own_ref[:, columns], ref[:, part * BLOCK : (part + 1) * BLOCK]

                acc_ref[...] = coded(own_hidden[...], values) + coded(received, other)
                keep_ref[0, :, columns] = acc_ref[mine, :].astype(jnp.bfloat16)
                send_ref[0, :, columns] = acc_ref[theirs, :].astype(jnp.bfloat16)

    out = jax.ShapeDtypeStruct((2, rows, width), jnp.bfloat16)
    part_spec = block_spec((tokens, piece), lambda i, p: (0, chunk % (CHUNKS // GROUPS)))
    return chain(
        f"g1{chunk}",
        body,
        (2,),
        [block_spec((units, tokens), lambda i, p: (i, 0))]
        + [whole((units, tokens))] * 2
        + [block_spec((tokens, width), lambda i, p: (0, chunk))]
        + [part_spec] * 4
        + [block_spec((2 * rows, block_count), lambda i, p: (i, 0))],
        [block_spec((1, rows, width), lambda i, p: (jnp.bitwise_xor(i, p[2]), 0, 0))] * 2,
        [out, out],
        [pltpu.VMEM((2 * rows, BLOCK), jnp.float32)],
        (*hidden_parts, rotated, *pieces, scales),
    )


def adam(chain, chunk, kept, received, shard_scales, flips, matrix, master, one, two, previous):
    rows, width = kept.shape
    model_width = master.shape[1]
    block_count = shard_scales.shape[1]
    step = width // ADAM_STEPS
    parts = step // BLOCK
    chained = previous is not None

    def body(place_ref, kept_ref, received_ref, scales_ref, flips_ref, matrix_ref, master_ref, one_ref, two_ref, *rest):
        grad_out, master_out, one_out, two_out, weight_out = rest[-5:]
        lane = lax.broadcasted_iota(jnp.int32, (rows, block_count), 1)
        all_scales = scales_ref[...]
        for part in range(parts):
            block = (chunk * ADAM_STEPS + pl.program_id(0)) * parts + part
            columns = slice(part * BLOCK, (part + 1) * BLOCK)
            scale = jnp.sum(jnp.where(lane == block, all_scales, 0.0), axis=1, keepdims=True)
            decoded = dot(kept_ref[:, columns], matrix_ref[...]) + dot(received_ref[:, columns], matrix_ref[...])
            gradient = decoded / scale * flips_ref[part]
            new_one = BETA_ONE * one_ref[:, columns] + (1.0 - BETA_ONE) * gradient
            new_two = BETA_TWO * two_ref[:, columns] + (1.0 - BETA_TWO) * gradient * gradient
            update = new_one / FIRST_BIAS / (jnp.sqrt(new_two / SECOND_BIAS) + EPSILON)
            old = master_ref[:, columns]
            new_master = old - LEARN_RATE * (update + WEIGHT_DECAY * old)
            grad_out[:, columns] = gradient
            master_out[:, columns] = new_master
            one_out[:, columns] = new_one
            two_out[:, columns] = new_two
            weight_out[:, columns] = new_master.astype(jnp.bfloat16)

    local = block_spec((rows, step), lambda j, p: (0, j))
    placed = block_spec((rows, step), lambda j, p: (0, chunk * ADAM_STEPS + j))
    state = jax.ShapeDtypeStruct((rows, model_width), jnp.float32)
    return chain(
        f"ad{chunk}",
        body,
        (ADAM_STEPS,),
        [
            local,
            local,
            whole((rows, block_count)),
            block_spec((parts, 1, BLOCK), lambda j, p: (chunk * ADAM_STEPS + j, 0, 0)),
            whole((BLOCK, BLOCK)),
            placed,
            placed,
            placed,
        ]
        + ([pl.BlockSpec(memory_space=pl.ANY)] * 4 if chained else []),
        [placed] * 4 + [local],
        [state] * 4 + [jax.ShapeDtypeStruct((rows, width), jnp.bfloat16)],
        [],
        (
            kept,
            received,
            shard_scales,
            flips.astype(jnp.float32).reshape(block_count, 1, BLOCK),
            matrix,
            *(pltpu.with_memory_space_constraint(value, pltpu.HBM) for value in (master, one, two)),
            *(previous if chained else ()),
        ),
        {9 + i: i for i in range(4)} if chained else None,
        token=4,
    )


def forward(chain, name, inputs, weight, other):
    tokens, units = inputs[0].shape
    rows, width = weight.shape
    quarter = tokens // 4
    step = width // FORWARD_STEPS

    def body(place_ref, n0, n1, n2, n3, weight_ref, other_ref, o0, o1, o2, o3, acc_ref, joined_ref):
        position, y = place_ref[0], place_ref[1]
        joined_ref[pl.ds(pl.multiple_of(y * rows, 8), rows), :] = weight_ref[...].astype(jnp.float32)
        joined_ref[pl.ds(pl.multiple_of((1 - y) * rows, 8), rows), :] = other_ref[...].astype(jnp.float32)
        joined = joined_ref[...].astype(jnp.bfloat16)
        for k, ref in enumerate((n0, n2, n1, n3)):
            acc_ref[...] = dot(ref[...], joined).astype(jnp.bfloat16)
            for i, out_ref in enumerate((o0, o1, o2, o3)):
                start = jnp.bitwise_xor(position, i) * quarter
                out_ref[k] = acc_ref[pl.ds(pl.multiple_of(start, quarter), quarter), :]

    return chain(
        name,
        body,
        (FORWARD_STEPS,),
        [whole((tokens, units))] * 4 + [block_spec((rows, step), lambda j, p: (0, j))] * 2,
        [block_spec((4, quarter, step), lambda j, p: (0, 0, j))] * 4,
        [jax.ShapeDtypeStruct((4, quarter, width), jnp.bfloat16)] * 4,
        [pltpu.VMEM((tokens, step), jnp.bfloat16), pltpu.VMEM((units, step), jnp.float32)],
        (*inputs, weight, other),
    )


def add(a, b):
    return (a.astype(jnp.float32) + b.astype(jnp.float32)).astype(jnp.bfloat16)


def on_device(
    hidden, next_hidden, out_grad, sign_bits, scale_index, master, moment_one, moment_two
):
    dp_size = lax.axis_size("dp")
    tensor_size = lax.axis_size("tensor")
    tokens = hidden.shape[0]
    shard_rows = master.shape[0]
    block_count = sign_bits.shape[0]
    replica = lax.axis_index("dp")
    group = lax.axis_index("tensor")
    z, y = replica // 2, replica % 2
    far_side = replica // 4
    place = jnp.stack([group, y, far_side]).astype(jnp.int32)
    matrix = jnp.asarray(hadamard(BLOCK)).astype(jnp.bfloat16)
    flips = (1 - 2 * sign_bits).astype(jnp.bfloat16)

    def over_dp(value, bits):
        return lax.ppermute(value, "dp", [(i, i ^ bits) for i in range(dp_size)])

    def over_tensor(value, bits):
        return lax.ppermute(value, "tensor", [(i, i ^ bits) for i in range(tensor_size)])

    units = 2 * shard_rows
    near_z = z % 2
    by_pair = hidden.T.reshape(2, 2, units, tokens)

    def pair_rows(values, k):
        picked = lax.dynamic_index_in_dim(values, near_z ^ k, 1, keepdims=False)
        return picked.reshape(2 * units, picked.shape[-1])

    hidden_parts = [pair_rows(by_pair, 0)] + [
        over_dp(lax.dynamic_index_in_dim(half, 1 - near_z, 0, keepdims=False), 2) for half in by_pair
    ]
    chain = Chain(place)
    rotated, *own_pieces = rotate(chain, out_grad, flips, matrix)

    level_table = jnp.array(LEVELS, jnp.float32)
    matches = (scale_index[:, :, None] == jnp.arange(4, dtype=jnp.int32)).astype(jnp.float32)
    all_scales = jnp.sum(matches * level_table, axis=-1) * math.sqrt(dp_size)
    scales = pair_rows(all_scales.reshape(2, 2, units, block_count), 0)
    shard_scales = lax.dynamic_slice_in_dim(scales, (2 * far_side + y) * shard_rows, shard_rows, 0)

    next_t = next_hidden.T
    inputs = [lax.dynamic_slice_in_dim(next_t, (z ^ k) * units, units, 0) for k in range(4)]
    inputs = [inputs[0]] + [over_dp(inputs[k], 2 * k) for k in range(1, 4)]

    state = None
    pieces, kept, halves, arriving, weights, partials, sums, nears, outs = ({} for _ in range(9))
    turned_inputs = {}

    def gather(k):
        u = over_dp(own_pieces[k], 2)
        v = over_tensor(u, 2)
        pieces[k] = (u, over_tensor(u, 1), v, over_tensor(v, 1))

    def first(k):
        kept[k], sent = coded_sum(chain, k, hidden_parts, rotated, pieces[k // (CHUNKS // GROUPS)], scales)
        halves[k] = over_dp(sent, 1)

    def join_rows(k):
        go = add(kept[k][1], halves[k][1])
        kept[k] = add(kept[k][0], halves[k][0])
        arriving[k] = over_dp(go, 4)
        chain.note(go)

    def update(k):
        nonlocal state
        *state, weight = adam(
            chain, k, kept[k], arriving[k], shard_scales, flips, matrix, master, moment_one, moment_two, state
        )
        weights[k] = (weight, over_dp(weight, 1))

    def turn(k):
        turned_inputs[k] = inputs[k].T
        chain.note(inputs[k])

    def second(k):
        stay, near, go, far = forward(chain, f"g2{k}", [turned_inputs[i] for i in range(4)], *weights[k])
        partials[k] = (stay, go, over_tensor(near, 1), over_tensor(far, 1))

    def sum_cores(k):
        stay, go, near, far = partials[k]
        go = add(go, far)
        sums[k] = (add(stay, near), over_tensor(go, 2))
        chain.note(go)

    def sum_chips(k):
        stay, more = sums[k]
        go = add(stay[2:], more[2:])
        nears[k] = (add(stay[:2], more[:2]), over_dp(go, 2))
        chain.note(go)

    def sum_near(k):
        stay, more = nears[k]
        go = add(stay[1], more[1])
        outs[k] = (add(stay[0], more[0]), over_dp(go, 4))
        chain.note(go)

    steps = {"tu": turn, "ay": join_rows, "g1": first, "ad": update, "g2": second, "sc": sum_cores, "sx": sum_chips, "sn": sum_near}
    for group_index in range(GROUPS):
        gather(group_index)
    for name in ORDER[1:]:
        steps[name[:2]](int(name[2:]))
    next_out = jnp.concatenate([add(*outs[k]) for k in range(CHUNKS)], axis=1)
    gradient, new_master, new_one, new_two = state
    return (gradient, new_master, new_one, new_two, next_out)


def general(
    hidden, next_hidden, out_grad, sign_bits, scale_index, master, moment_one, moment_two
):
    dp_size = lax.axis_size("dp")
    tok_rows = hidden.shape[0]
    model_width = out_grad.shape[1]
    block_count = sign_bits.shape[0]
    shard_rows = master.shape[0]
    matrix = jnp.asarray(hadamard(BLOCK))
    sign_flips = (1 - 2 * sign_bits).astype(jnp.float32)
    signed = out_grad.reshape(tok_rows, block_count, BLOCK) * sign_flips.astype(jnp.bfloat16)
    rotated = jnp.einsum(
        "tbj,jk->tbk", signed, matrix.astype(jnp.bfloat16), preferred_element_type=jnp.float32
    )
    rotated = rotated.astype(jnp.bfloat16).reshape(tok_rows, model_width)
    level_table = jnp.array(LEVELS, jnp.float32)
    matches = (scale_index[:, :, None] == jnp.arange(4, dtype=jnp.int32)).astype(jnp.float32)
    scales = jnp.sum(matches * level_table, axis=-1) * math.sqrt(dp_size)
    product = lax.dot_general(
        hidden, rotated, (((0,), (0,)), ((), ())), preferred_element_type=jnp.float32
    )
    scaled = product.reshape(dp_size * shard_rows, block_count, BLOCK) * scales[:, :, None]
    summed = lax.psum_scatter(
        jnp.clip(scaled, -CLIP_LEVEL, CLIP_LEVEL)
        .reshape(dp_size * shard_rows, model_width)
        .astype(jnp.bfloat16),
        "dp",
        scatter_dimension=0,
        tiled=True,
    ).astype(jnp.float32)
    shard_scales = lax.dynamic_slice_in_dim(
        scales, lax.axis_index("dp") * shard_rows, shard_rows, 0
    )
    unscaled = summed.reshape(shard_rows, block_count, BLOCK) / shard_scales[:, :, None]
    decoded = jnp.einsum("rbj,jk->rbk", unscaled, matrix, precision=lax.Precision.HIGHEST)
    gradient = (decoded * sign_flips).reshape(shard_rows, model_width)
    new_one = BETA_ONE * moment_one + (1.0 - BETA_ONE) * gradient
    new_two = BETA_TWO * moment_two + (1.0 - BETA_TWO) * gradient * gradient
    update = new_one / FIRST_BIAS / (jnp.sqrt(new_two / SECOND_BIAS) + EPSILON)
    new_master = master - LEARN_RATE * (update + WEIGHT_DECAY * master)
    partial_value = jnp.dot(
        next_hidden,
        lax.all_gather(new_master.astype(jnp.bfloat16), "dp", axis=0, tiled=True),
        preferred_element_type=jnp.float32,
    )
    next_out = lax.psum_scatter(
        partial_value.astype(jnp.bfloat16), "tensor", scatter_dimension=0, tiled=True
    )
    return (gradient, new_master, new_one, new_two, next_out)


def solution(mesh):
    grouped = mesh.shape["dp"] == 8 and mesh.shape["tensor"] == 4
    return jax.shard_map(
        on_device if grouped else general,
        mesh=mesh,
        in_specs=(
            P("dp", "tensor"),
            P("dp", "tensor"),
            P("dp", None),
            P(),
            P("tensor", None),
            P(("tensor", "dp"), None),
            P(("tensor", "dp"), None),
            P(("tensor", "dp"), None),
        ),
        out_specs=(
            P(("tensor", "dp"), None),
            P(("tensor", "dp"), None),
            P(("tensor", "dp"), None),
            P(("tensor", "dp"), None),
            P(("dp", "tensor"), None),
        ),
        check_vma=False,
    )
```
